1024 devices in a mesh: mid: 128 (over y, z), off: 8 (over x, core).
Axes of the slice: x: 4, y: 8, z: 16, core: 2. Of those that a mesh axis runs over, the one named last changes fastest.
Arguments:
- traces: bfloat16 [131072, 512], P(('mid', 'off')), may hold values from -16 to 16
- kernels: bfloat16 [8, 512, 512], replicated, may hold values from -0.25 to 0.25
- send_list: int32 [128, 4, 4], P('mid'), may hold values from 0 to 7, as said below
- aper_slot: int32 [8, 131072], P(None, ('mid', 'off')), may hold values from 0 to 23, as said below
- aper_pattern: int32 [8, 131072], P(None, ('mid', 'off')), may hold values from 0 to 7
- trace_bin: int32 [131072], P(('mid', 'off')), may hold values from 0 to 7
- trace_count: int32 [131072], P(('mid', 'off')), may hold values from 5 to 8, as said below
Outputs:
- solution: float32 [1024, 64, 512], P('mid', 'off')
- residual: float32 [1024, 64, 512], P('mid', 'off')
The draws below stay inside these ranges and needn't reach their ends.
Inputs may be any that keep to these rules, and one draw needn't show every extreme that they name: Each row send_list[i, k, :] holds 4 different cells of tile i. `aper_slot`: with r = j % 5, entry j of every list names one of the 8 own cells of the trace's tile when r == 0, and otherwise one of slots 8 + (r - 1) * 4 to 8 + r * 4 - 1, the cells that arrive from direction r - 1. Only the first trace_count[t] entries of a list are live.
All inputs are finite; a program needn't handle non-finite values.
Results may differ from the reference program's by a relative error of at most 0.015.
Values may be sent and summed in bfloat16 or wider, within the bound.
A program may use at most 32 MiB of HBM per device.

```python
import jax
import jax.numpy as jnp
from jax import lax

NT = 512
NOFF = 64
PATTERNS = 8
REACH = 2
APER = 8
ITERS = 2
CELLS = 8
SEND = 4
TR_DEV = 128
TILES = 128
OFF_DEV = 8
TRACES = 131072
DIRS = 4
SLOTS = 24
N_MID = 128
N_OFF = 8


def draw_traces(key, part):
    key = jax.random.fold_in(key, 11)
    rising = jnp.arange(TRACES, dtype=jnp.float32) / (TRACES - 1)
    values = jnp.clip(jax.random.normal(key, (TRACES, NT), jnp.float32), -4.0, 4.0)
    row_scale = 1.0 + 2.0 * rising
    return (values * row_scale[:, None]).astype(jnp.bfloat16)


def draw_send_list(key, part):
    key = jax.random.fold_in(key, 12)
    scores = jax.random.randint(key, (TILES, DIRS, CELLS), 0, 1 << 20) * CELLS + jnp.arange(CELLS, dtype=jnp.int32)
    return jnp.argsort(scores, axis=-1)[:, :, :SEND].astype(jnp.int32)


def draw_aper_slot(key, part):
    key = jax.random.fold_in(key, 13)
    region = jnp.arange(APER, dtype=jnp.int32) % (DIRS + 1)
    region_base = jnp.where(region == 0, 0, CELLS + (region - 1) * SEND)
    region_size = jnp.where(region == 0, CELLS, SEND)
    random_bits = jax.random.randint(key, (APER, TRACES), 0, 1 << 20)
    slot_ids = region_base[:, None] + random_bits % region_size[:, None]
    slot_ids = slot_ids.at[0, 0].set(0).at[DIRS, 0].set(SLOTS - 1)
    return slot_ids.astype(jnp.int32)


def draw_trace_count(key, part):
    key = jax.random.fold_in(key, 14)
    groups = NOFF // OFF_DEV
    trace_ids = jnp.arange(TRACES, dtype=jnp.int32)
    upper_half = trace_ids // TR_DEV % groups >= groups // 2
    flipped = jax.random.randint(key, (TRACES,), 0, 8) == 0
    fewest = 2 * REACH + 1
    lower_counts = jnp.where(flipped, fewest + 1, fewest)
    upper_counts = jnp.where(flipped, max(APER - 1, fewest), APER)
    counts = jnp.where(upper_half, upper_counts, lower_counts)
    counts = counts.at[0].set(fewest).at[TRACES - 1].set(APER)
    return counts.astype(jnp.int32)


def touch_ends(drawn, rng, least, high):
    place = [jax.random.randint(jax.random.fold_in(rng, axis), (), 0, length) for axis, length in enumerate(drawn.shape)]
    widest = drawn.shape.index(max(drawn.shape))
    neighbour = place[:widest] + [(place[widest] + 1) % drawn.shape[widest]] + place[widest + 1:]
    return drawn.at[tuple(place)].set(least).at[tuple(neighbour)].set(high)


def bell_draw(key, shape, scale, limit, kind=jnp.bfloat16):
    values = jax.random.normal(key, shape, jnp.float32) * scale
    return jnp.minimum(jnp.maximum(values, -limit), limit).astype(kind)


def setup_inputs(seed: int = 0) -> dict:
    arg_keys = jax.random.split(jax.random.key(seed), 8)
    return {
        "traces": draw_traces(jax.random.fold_in(arg_keys[7], 71), 0),
        "kernels": bell_draw(arg_keys[1], (PATTERNS, NT, NT), NT ** -0.5, 0.25),
        "send_list": draw_send_list(jax.random.fold_in(arg_keys[7], 71), 0),
        "aper_slot": draw_aper_slot(jax.random.fold_in(arg_keys[7], 71), 0),
        "aper_pattern": touch_ends(jax.random.randint(arg_keys[4], (APER, TRACES), 0, PATTERNS), jax.random.fold_in(arg_keys[4], 1), 0, PATTERNS - 1).astype(jnp.int32),
        "trace_bin": touch_ends(jax.random.randint(arg_keys[5], (TRACES,), 0, OFF_DEV), jax.random.fold_in(arg_keys[5], 1), 0, OFF_DEV - 1).astype(jnp.int32),
        "trace_count": draw_trace_count(jax.random.fold_in(arg_keys[7], 71), 0),
    }


smooth_weight = 2.0


def direction_shift(course):
    return (course // 2 + 1) * (1 - 2 * (course % 2))


def cell_lookup(send_list):
    tile_ids = jnp.arange(N_MID, dtype=jnp.int32)
    own_cells = tile_ids[:, None] * CELLS + jnp.arange(CELLS, dtype=jnp.int32)[None, :]
    columns_list = [own_cells]
    for course in range(2 * REACH):
        source = tile_ids - direction_shift(course)
        valid_mask = (source >= 0) & (source < N_MID)
        safe_source = jnp.clip(source, 0, N_MID - 1).astype(jnp.int32)
        cell_ids = safe_source[:, None] * CELLS + send_list[safe_source, course, :]
        columns_list.append(jnp.where(valid_mask[:, None], cell_ids, CELLS * N_MID))
    return jnp.concatenate(columns_list, axis=1).astype(jnp.int32)


def entry_tables(send_list, aper_slot, trace_bin, trace_count):
    lookup = cell_lookup(send_list)
    trace_ids = jnp.arange(TR_DEV * N_MID * N_OFF, dtype=jnp.int32)
    tile_index = trace_ids // (TR_DEV * N_OFF)
    offset_bin = ((trace_ids // TR_DEV) % N_OFF) * (NOFF // N_OFF) + trace_bin
    cell_index = lookup[tile_index[None, :], aper_slot]
    valid_mask = (cell_index < CELLS * N_MID) & (jnp.arange(APER, dtype=jnp.int32)[:, None] < trace_count[None, :])
    entry_index = jnp.where(valid_mask, cell_index * NOFF + offset_bin[None, :], CELLS * N_MID * NOFF)
    return entry_index.astype(jnp.int32), valid_mask


def by_tiles(array):
    return jnp.transpose(array.reshape(array.shape[0], N_MID, -1), (1, 0, 2))


def forward_tile(flat_field, kernels, entry_index, valid_mask, patterns):
    safe_index = jnp.where(valid_mask, entry_index, 0).astype(jnp.int32)
    blocks = flat_field[safe_index].astype(jnp.float32) * valid_mask[..., None].astype(jnp.float32)
    chooser = (patterns[None] == jnp.arange(PATTERNS, dtype=jnp.int32)[:, None, None]).astype(jnp.float32)
    pattern_sums = jnp.einsum("pjt,jtn->ptn", chooser, blocks).astype(jnp.bfloat16)
    return jnp.einsum("ptn,pnm->tm", pattern_sums.astype(jnp.float32), kernels.astype(jnp.float32))


def adjoint_tile(accumulated, values, entry_index, valid_mask, patterns, kernels):
    spread = jnp.einsum("tm,pnm->ptn", values.astype(jnp.float32), kernels.astype(jnp.float32))
    chooser = (patterns[None] == jnp.arange(PATTERNS, dtype=jnp.int32)[:, None, None]).astype(jnp.float32)
    chooser = chooser * valid_mask[None].astype(jnp.float32)
    entries = jnp.einsum("pjt,ptn->jtn", chooser, spread)
    return accumulated.at[entry_index.reshape(-1)].add(entries.reshape(-1, NT), mode="drop")


def smoothing(field):
    padded = jnp.pad(field, ((0, 0), (1, 1), (0, 0)))
    return smooth_weight * (2.0 * field - padded[:, :-2] - padded[:, 2:])


def reference(traces, kernels, send_list, aper_slot, aper_pattern, trace_bin, trace_count):
    entry_index, valid_mask = entry_tables(send_list, aper_slot, trace_bin, trace_count)
    tiled = (by_tiles(entry_index), by_tiles(valid_mask), by_tiles(aper_pattern))
    model_rows = CELLS * N_MID * NOFF
    model_shape = (CELLS * N_MID, NOFF, NT)

    def adjoint_all(values_tiled):
        def advance(accumulated, pieces):
            values, index_tile, mask_tile, pattern_tile = pieces
            return adjoint_tile(accumulated, values, index_tile, mask_tile, pattern_tile, kernels), None
        accumulated, _ = lax.scan(advance, jnp.zeros((model_rows, NT), jnp.float32), (values_tiled,) + tiled)
        return accumulated.reshape(model_shape)

    def normal_all(field):
        flat_field = field.astype(jnp.bfloat16).reshape(model_rows, NT)

        def advance(accumulated, pieces):
            index_tile, mask_tile, pattern_tile = pieces
            applied = forward_tile(flat_field, kernels, index_tile, mask_tile, pattern_tile).astype(jnp.bfloat16)
            return adjoint_tile(accumulated, applied, index_tile, mask_tile, pattern_tile, kernels), None
        accumulated, _ = lax.scan(advance, jnp.zeros((model_rows, NT), jnp.float32), tiled)
        return accumulated.reshape(model_shape) + smoothing(field)

    residual = adjoint_all(traces.reshape(N_MID, N_OFF * TR_DEV, NT))
    direction = residual
    solution = jnp.zeros_like(residual)
    norm_now = jnp.sum(residual * residual)
    for iteration in range(ITERS):
        applied = normal_all(direction)
        step_size = norm_now / jnp.sum(direction * applied)
        solution = solution + step_size * direction
        residual = residual - step_size * applied
        if iteration + 1 < ITERS:
            norm_next = jnp.sum(residual * residual)
            direction = residual + (norm_next / norm_now) * direction
            norm_now = norm_next
    return solution, residual
```

```python
import functools

import jax
import jax.numpy as jnp
from jax import lax
from jax.experimental import pallas as pl
from jax.experimental.pallas import tpu as pltpu
from jax.sharding import PartitionSpec as P

MESH = pl.DeviceIdType.MESH
PATTERNS = 8
APER = 8
CELLS = 8
SEND = 4
DIRS = 4
BINS = 8
OWN = CELLS * BINS
PART = SEND * BINS
AWAY = DIRS * PART
ROWS = OWN + AWAY
CHUNKS = 2
SHIFTS = (1, -1, 2, -2)
FAR_FIRST = (2, 3, 0, 1)
smooth_weight = 2.0
F32 = jnp.float32
BF16 = jnp.bfloat16


def dot(a, b):
    return jnp.dot(a, b, preferred_element_type=F32)


def dot_t(a, b):
    return lax.dot_general(a, b, (((1,), (1,)), ((), ())), preferred_element_type=F32)


def by_lanes(x):
    rows, n = x.shape
    x = x.reshape(rows // 8, 8, n).sum(0)
    x = sum(x[:, i : i + 128] for i in range(0, n, 128))
    return jnp.sum(x, axis=0, keepdims=True)


def body(
    sizes,
    traces_ref,
    kernels_ref,
    send_ref,
    slot_ref,
    pattern_ref,
    bin_ref,
    count_ref,
    solution_ref,
    residual_ref,
    moveout,
    pick,
    spread_to,
    spread,
    own,
    back_send,
    back_land,
    slots,
    ahead_send,
    field0,
    field1,
    smooth,
    edge_send,
    edge_land,
    totals,
    total_send,
    total_a,
    total_b,
    total_c,
    load_sem,
    back_ssem,
    back_rsem,
    ahead_ssem,
    ahead_rsem,
    edge_ssem,
    edge_rsem,
    total_ssem,
    total_rsem,
):
    n_mid, n_off, n_z = sizes
    n_y = n_mid // n_z
    samples = moveout.shape[2]
    trace_rows = traces_ref.shape[0]
    width = samples // CHUNKS
    mid = lax.axis_index("mid")
    off = lax.axis_index("off")
    row_y = lax.div(mid, n_z)
    col_z = lax.rem(mid, n_z)

    def tile_at(shift):
        return lax.rem(mid + (shift + n_mid), n_mid)

    tiles_to = [tile_at(s) for s in SHIFTS]
    tiles_back = [tile_at(-s) for s in SHIFTS]
    off_peers = [lax.rem(off + d, n_off) for d in range(1, n_off)]
    z_peers = [row_y * n_z + lax.rem(col_z + d, n_z) for d in range(1, n_z)]
    y_peers = [lax.rem(row_y + d, n_y) * n_z + col_z for d in range(1, n_y)]

    loads = [
        pltpu.make_async_copy(kernels_ref.at[p], moveout.at[p], load_sem.at[p]) for p in range(PATTERNS)
    ]
    for load in loads:
        load.start()

    barrier = pltpu.get_barrier_semaphore()
    greeted = 0
    for tile in tiles_to + z_peers + y_peers:
        pl.semaphore_signal(barrier, inc=1, device_id=(tile, off), device_id_type=MESH)
        greeted += 1
    for peer in off_peers:
        pl.semaphore_signal(barrier, inc=1, device_id=(mid, peer), device_id_type=MESH)
        greeted += 1

    slot = slot_ref[...]
    live = lax.broadcasted_iota(jnp.int32, slot.shape, 0) < count_ref[...].reshape(1, trace_rows)
    for k in range(DIRS):
        source = mid - SHIFTS[k]
        here = (source >= 0) & (source < n_mid)
        inside = (slot >= CELLS + k * SEND) & (slot < CELLS + (k + 1) * SEND)
        live = live & (jnp.logical_not(inside) | here)
    code = pattern_ref[...] * ROWS + slot * BINS + bin_ref[...].reshape(1, trace_rows)
    code = jnp.where(live, code, -1)
    row_id = lax.broadcasted_iota(jnp.int32, (ROWS, trace_rows), 0)
    for p in range(PATTERNS):
        count = jnp.zeros((ROWS, trace_rows), F32)
        for j in range(APER):
            count = count + jnp.where(code[j : j + 1, :] - p * ROWS == row_id, 1.0, 0.0)
        spread_to[:, p * trace_rows : (p + 1) * trace_rows] = count.astype(BF16)
        pick[p * trace_rows : (p + 1) * trace_rows, :] = count.T.astype(BF16)

    entry = lax.broadcasted_iota(jnp.int32, (OWN, AWAY), 1)
    listed = jnp.zeros((OWN, AWAY), jnp.int32)
    for k in range(DIRS):
        for m in range(SEND):
            listed = jnp.where(entry // BINS == k * SEND + m, send_ref[0, k, m], listed)
    place = listed * BINS + entry % BINS
    land_f32 = jnp.where(place == lax.broadcasted_iota(jnp.int32, (OWN, AWAY), 0), 1.0, 0.0)
    land_at = land_f32.astype(BF16)
    take_from = land_f32.T.astype(BF16)

    def cols(c):
        return slice(c * width, (c + 1) * width)

    def back_copy(turn, c, k):
        part = pl.ds(k * PART, PART)
        return pltpu.make_async_remote_copy(
            src_ref=back_send.at[turn, c, part, :],
            dst_ref=back_land.at[turn, c, part, :],
            send_sem=back_ssem.at[turn, c],
            recv_sem=back_rsem.at[turn, c],
            device_id=(tiles_back[k], off),
            device_id_type=MESH,
        )

    def ahead_copy(turn, c, k):
        return pltpu.make_async_remote_copy(
            src_ref=ahead_send.at[turn, c, pl.ds(k * PART, PART), :],
            dst_ref=slots.at[turn, c, pl.ds(OWN + k * PART, PART), :],
            send_sem=ahead_ssem.at[turn, c],
            recv_sem=ahead_rsem.at[turn, c],
            device_id=(tiles_to[k], off),
            device_id_type=MESH,
        )

    def edge_copy(turn, side):
        step = 1 - 2 * side
        return pltpu.make_async_remote_copy(
            src_ref=edge_send.at[turn, side],
            dst_ref=edge_land.at[turn, side],
            send_sem=edge_ssem.at[turn, side],
            recv_sem=edge_rsem.at[turn, side],
            device_id=(mid, lax.rem(off + step + n_off, n_off)),
            device_id_type=MESH,
        )

    def await_bytes(ref, sem):
        pltpu.make_async_copy(ref, ref, sem).wait()

    def adjoint_chunk(turn, c, values, first=False):
        for p in range(PATTERNS):
            if first and c == 0:
                loads[p].wait()
            part = dot_t(values, moveout[p, cols(c), :])
            spread[p * trace_rows : (p + 1) * trace_rows, :] = part.astype(BF16)
        sums = dot(spread_to[...], spread[...])
        own[c] = sums[:OWN]
        back_send[turn, c] = sums[OWN:].astype(BF16)
        if first and c == 0:
            pl.semaphore_wait(barrier, greeted)
        for k in FAR_FIRST:
            back_copy(turn, c, k).start()

    def landed(turn, c):
        await_bytes(back_land.at[turn, c], back_rsem.at[turn, c])
        return own[c] + dot(land_at, back_land[turn, c])

    def ahead_chunk(turn, c, part):
        rounded = part.astype(BF16)
        ahead_send[turn, c] = dot(take_from, rounded).astype(BF16)
        for k in FAR_FIRST:
            ahead_copy(turn, c, k).start()
        slots[turn, c, :OWN, :] = rounded

    def send_edges(turn, field):
        cube = field[...].reshape(CELLS, BINS, samples)
        edge_send[turn, 0] = cube[:, BINS - 1, :]
        edge_send[turn, 1] = cube[:, 0, :]
        for side in range(2):
            edge_copy(turn, side).start()

    def smoothed(turn, field):
        for side in range(2):
            await_bytes(edge_land.at[turn, side], edge_rsem.at[turn, side])
        before = jnp.where(off == 0, 0.0, edge_land[turn, 0])
        after = jnp.where(off == n_off - 1, 0.0, edge_land[turn, 1])
        cube = field[...].reshape(CELLS, BINS, samples)
        padded = jnp.concatenate([before[:, None, :], cube, after[:, None, :]], axis=1)
        out = smooth_weight * (2.0 * cube - padded[:, :-2] - padded[:, 2:])
        return out.reshape(OWN, samples)

    def forward(turn):
        out = jnp.zeros((trace_rows, samples), F32)
        for c in range(CHUNKS):
            await_bytes(slots.at[turn, c, pl.ds(OWN, AWAY), :], ahead_rsem.at[turn, c])
            sums = dot(pick[...], slots[turn, c]).astype(BF16)
            for p in range(PATTERNS):
                out = out + dot(sums[p * trace_rows : (p + 1) * trace_rows], moveout[p, cols(c), :])
        return out

    def total_copies(turn, stage):
        land, where = stages[stage]
        return [
            pltpu.make_async_remote_copy(
                src_ref=total_send.at[turn, stage],
                dst_ref=land.at[turn, d],
                send_sem=total_ssem.at[turn, stage],
                recv_sem=total_rsem.at[turn, stage],
                device_id=device,
                device_id_type=MESH,
            )
            for d, device in enumerate(where)
        ]

    stages = [
        (total_a, [(mid, peer) for peer in off_peers]),
        (total_b, [(tile, off) for tile in z_peers]),
        (total_c, [(tile, off) for tile in y_peers]),
    ]

    def total_start(turn, stage, mine):
        total_send[turn, stage] = mine
        for copy in total_copies(turn, stage):
            copy.start()

    def total_end(turn, stage):
        land = stages[stage][0]
        await_bytes(land.at[turn], total_rsem.at[turn, stage])
        return total_send[turn, stage] + jnp.sum(land[turn], axis=0)

    values = traces_ref[...]
    for c in range(CHUNKS):
        adjoint_chunk(0, c, values, first=True)
    norm = jnp.zeros((1, 128), F32)
    for c in range(CHUNKS):
        part = landed(0, c)
        ahead_chunk(0, c, part)
        field0[:, cols(c)] = part
        norm = norm + by_lanes(part * part)

    for turn, field in ((0, field0), (1, field1)):
        send_edges(turn, field)
        smooth[...] = smoothed(turn, field)
        cross = by_lanes(field[...] * smooth[...])
        values = forward(turn).astype(BF16)
        heard = values.astype(F32)
        totals[0:1, :] = norm
        totals[1:2, :] = by_lanes(heard * heard) + cross
        totals[2:8, :] = jnp.zeros((6, 128), F32)
        total_start(turn, 0, totals[...])
        for c in range(CHUNKS):
            adjoint_chunk(turn + 1, c, values)
            if c < 2:
                total_start(turn, c + 1, total_end(turn, c))
        sums = jnp.sum(total_end(turn, 2), axis=1, keepdims=True)
        if turn == 0:
            norm_0 = sums[0:1, :]
            step_0 = norm_0 / sums[1:2, :]
            norm = jnp.zeros((1, 128), F32)
            for c in range(CHUNKS):
                part = field0[:, cols(c)] - step_0 * (landed(1, c) + smooth[:, cols(c)])
                ahead_chunk(1, c, part)
                field1[:, cols(c)] = part
                norm = norm + by_lanes(part * part)
        else:
            norm_1 = sums[0:1, :]
            ratio = norm_1 / norm_0
            step_1 = norm_1 / (sums[1:2, :] - ratio * (norm_1 / step_0))
            older = step_1 * ratio
            for c in range(CHUNKS):
                r, q = field0[:, cols(c)], field1[:, cols(c)]
                image = landed(2, c) + smooth[:, cols(c)]
                cube = (CELLS, BINS, width)
                solution_ref[:, :, cols(c)] = ((step_0 + older) * r + step_1 * q).reshape(cube)
                residual_ref[:, :, cols(c)] = (q - step_1 * image - (older / step_0) * (r - q)).reshape(cube)

    for turn in range(3):
        for c in range(CHUNKS):
            await_bytes(back_send.at[turn, c], back_ssem.at[turn, c])
    for turn in range(2):
        for c in range(CHUNKS):
            await_bytes(ahead_send.at[turn, c], ahead_ssem.at[turn, c])
        for side in range(2):
            await_bytes(edge_send.at[turn, side], edge_ssem.at[turn, side])
        for stage in range(3):
            await_bytes(stages[stage][0].at[turn], total_ssem.at[turn, stage])


def shards(sizes, traces, kernels, send_list, aper_slot, aper_pattern, trace_bin, trace_count):
    n_mid, n_off, n_z = sizes
    n_y = n_mid // n_z
    trace_rows, samples = traces.shape
    width = samples // CHUNKS
    vmem = pl.BlockSpec(memory_space=pltpu.VMEM)
    shape = jax.ShapeDtypeStruct((CELLS, BINS, samples), F32)
    return pl.pallas_call(
        functools.partial(body, sizes),
        out_shape=(shape, shape),
        in_specs=[
            vmem,
            pl.BlockSpec(memory_space=pl.ANY),
            pl.BlockSpec(memory_space=pltpu.SMEM),
            vmem,
            vmem,
            vmem,
            vmem,
        ],
        out_specs=(vmem, vmem),
        scratch_shapes=[
            pltpu.VMEM((PATTERNS, samples, samples), BF16),
            pltpu.VMEM((PATTERNS * trace_rows, ROWS), BF16),
            pltpu.VMEM((ROWS, PATTERNS * trace_rows), BF16),
            pltpu.VMEM((PATTERNS * trace_rows, width), BF16),
            pltpu.VMEM((CHUNKS, OWN, width), F32),
            pltpu.VMEM((3, CHUNKS, AWAY, width), BF16),
            pltpu.VMEM((3, CHUNKS, AWAY, width), BF16),
            pltpu.VMEM((2, CHUNKS, ROWS, width), BF16),
            pltpu.VMEM((2, CHUNKS, AWAY, width), BF16),
            pltpu.VMEM((OWN, samples), F32),
            pltpu.VMEM((OWN, samples), F32),
            pltpu.VMEM((OWN, samples), F32),
            pltpu.VMEM((2, 2, CELLS, samples), F32),
            pltpu.VMEM((2, 2, CELLS, samples), F32),
            pltpu.VMEM((8, 128), F32),
            pltpu.VMEM((2, 3, 8, 128), F32),
            pltpu.VMEM((2, n_off - 1, 8, 128), F32),
            pltpu.VMEM((2, n_z - 1, 8, 128), F32),
            pltpu.VMEM((2, n_y - 1, 8, 128), F32),
            pltpu.SemaphoreType.DMA((PATTERNS,)),
            pltpu.SemaphoreType.DMA((3, CHUNKS)),
            pltpu.SemaphoreType.DMA((3, CHUNKS)),
            pltpu.SemaphoreType.DMA((2, CHUNKS)),
            pltpu.SemaphoreType.DMA((2, CHUNKS)),
            pltpu.SemaphoreType.DMA((2, 2)),
            pltpu.SemaphoreType.DMA((2, 2)),
            pltpu.SemaphoreType.DMA((2, 3)),
            pltpu.SemaphoreType.DMA((2, 3)),
        ],
        compiler_params=pltpu.CompilerParams(
            collective_id=0, has_side_effects=True, vmem_limit_bytes=40 * 2**20
        ),
        name="inversion",
    )(traces, kernels, send_list, aper_slot, aper_pattern, trace_bin, trace_count)


def solution(mesh):
    n_mid, n_off = mesh.shape["mid"], mesh.shape["off"]
    n_z = 16 if n_mid % 16 == 0 else 4
    in_specs = (
        P(("mid", "off"), None),
        P(),
        P("mid", None, None),
        P(None, ("mid", "off")),
        P(None, ("mid", "off")),
        P(("mid", "off")),
        P(("mid", "off")),
    )
    out_specs = (P("mid", "off", None), P("mid", "off", None))
    return jax.shard_map(
        functools.partial(shards, (n_mid, n_off, n_z)),
        mesh=mesh,
        in_specs=in_specs,
        out_specs=out_specs,
        check_vma=False,
    )
```

```python
import functools

import jax
import jax.numpy as jnp
from jax import lax
from jax.experimental import pallas as pl
from jax.experimental.pallas import tpu as pltpu
from jax.sharding import PartitionSpec as P

MESH = pl.DeviceIdType.MESH
PATTERNS = 8
APER = 8
CELLS = 8
SEND = 4
DIRS = 4
BINS = 8
OWN = CELLS * BINS
PART = SEND * BINS
AWAY = DIRS * PART
ROWS = OWN + AWAY
CHUNKS = 2
SHIFTS = (1, -1, 2, -2)
FAR_FIRST = (2, 3, 0, 1)
smooth_weight = 2.0
F32 = jnp.float32
BF16 = jnp.bfloat16


def dot(a, b):
    return jnp.dot(a, b, preferred_element_type=F32)


def dot_t(a, b):
    return lax.dot_general(a, b, (((1,), (1,)), ((), ())), preferred_element_type=F32)


def by_lanes(x):
    rows, n = x.shape
    x = x.reshape(rows // 8, 8, n).sum(0)
    x = sum(x[:, i : i + 128] for i in range(0, n, 128))
    return jnp.sum(x, axis=0, keepdims=True)


def body(
    sizes,
    traces_ref,
    kernels_ref,
    send_ref,
    slot_ref,
    pattern_ref,
    bin_ref,
    count_ref,
    solution_ref,
    residual_ref,
    moveout,
    traces_in,
    send_in,
    slot_in,
    pattern_in,
    bin_in,
    count_in,
    pick,
    spread_to,
    spread,
    own,
    back_send,
    back_land,
    slots,
    ahead_send,
    field0,
    field1,
    smooth,
    edge_send,
    edge_land,
    total_send,
    total_land,
    load_sem,
    table_sem,
    back_ssem,
    back_rsem,
    ahead_ssem,
    ahead_rsem,
    edge_ssem,
    edge_rsem,
    total_ssem,
    total_rsem,
):
    n_mid, n_off, n_z = sizes
    n_y, n_x = n_mid // n_z, n_off // 2
    samples = moveout.shape[2]
    trace_rows = traces_in.shape[0]
    width = samples // CHUNKS
    mid = lax.axis_index("mid")
    off = lax.axis_index("off")
    row_y, col_z = lax.div(mid, n_z), lax.rem(mid, n_z)
    col_x, core = lax.div(off, 2), lax.rem(off, 2)

    def tile_at(shift):
        return lax.rem(mid + (shift + n_mid), n_mid)

    tiles_to = [tile_at(s) for s in SHIFTS]
    tiles_back = [tile_at(-s) for s in SHIFTS]

    def farthest_first(sizes_2, where):
        pairs = [(i, j) for i in range(sizes_2[0]) for j in range(sizes_2[1]) if i or j]
        pairs.sort(key=lambda ij: -min(ij[0], sizes_2[0] - ij[0]) - min(ij[1], sizes_2[1] - ij[1]))
        return [where(i, j) for i, j in pairs]

    line = farthest_first(
        (n_z, 2), lambda i, j: (row_y * n_z + lax.rem(col_z + i, n_z), col_x * 2 + lax.rem(core + j, 2))
    )
    plane = farthest_first(
        (n_y, n_x),
        lambda i, j: (lax.rem(row_y + i, n_y) * n_z + col_z, lax.rem(col_x + j, n_x) * 2 + core),
    )
    stages = (line, plane)

    tables = [
        pltpu.make_async_copy(src, dst, table_sem.at[i])
        for i, (src, dst) in enumerate(
            (
                (slot_ref, slot_in),
                (pattern_ref, pattern_in),
                (bin_ref, bin_in),
                (count_ref, count_in),
                (send_ref, send_in),
                (traces_ref, traces_in),
            )
        )
    ]
    for load in tables:
        load.start()
    loads = [
        pltpu.make_async_copy(kernels_ref.at[p], moveout.at[p], load_sem.at[p]) for p in range(PATTERNS)
    ]
    for load in loads:
        load.start()

    barrier = pltpu.get_barrier_semaphore()
    greeted = [device for stage in stages for device in stage]
    greeted += [(tile, off) for tile in tiles_to]
    greeted += [(mid, lax.rem(off + 1, n_off)), (mid, lax.rem(off + n_off - 1, n_off))]
    for device in greeted:
        pl.semaphore_signal(barrier, inc=1, device_id=device, device_id_type=MESH)
    for load in tables:
        load.wait()

    slot = slot_in[...]
    live = lax.broadcasted_iota(jnp.int32, slot.shape, 0) < count_in[...].reshape(1, trace_rows)
    for k in range(DIRS):
        source = mid - SHIFTS[k]
        here = (source >= 0) & (source < n_mid)
        inside = (slot >= CELLS + k * SEND) & (slot < CELLS + (k + 1) * SEND)
        live = live & (jnp.logical_not(inside) | here)
    code = pattern_in[...] * ROWS + slot * BINS + bin_in[...].reshape(1, trace_rows)
    code = jnp.where(live, code, -1)
    row_id = lax.broadcasted_iota(jnp.int32, (ROWS, trace_rows), 0)
    for p in range(PATTERNS):
        count = jnp.zeros((ROWS, trace_rows), F32)
        for j in range(APER):
            count = count + jnp.where(code[j : j + 1, :] - p * ROWS == row_id, 1.0, 0.0)
        spread_to[:, p * trace_rows : (p + 1) * trace_rows] = count.astype(BF16)
        pick[p * trace_rows : (p + 1) * trace_rows, :] = count.T.astype(BF16)

    entry = lax.broadcasted_iota(jnp.int32, (OWN, AWAY), 1)
    listed = jnp.zeros((OWN, AWAY), jnp.int32)
    for k in range(DIRS):
        for m in range(SEND):
            listed = jnp.where(entry // BINS == k * SEND + m, send_in[0, k : k + 1, m : m + 1], listed)
    place = listed * BINS + entry % BINS
    land_f32 = jnp.where(place == lax.broadcasted_iota(jnp.int32, (OWN, AWAY), 0), 1.0, 0.0)
    land_at = land_f32.astype(BF16)
    take_from = land_f32.T.astype(BF16)

    def cols(c):
        return slice(c * width, (c + 1) * width)

    def back_copy(turn, c, k):
        part = pl.ds(k * PART, PART)
        return pltpu.make_async_remote_copy(
            src_ref=back_send.at[turn, c, part, :],
            dst_ref=back_land.at[turn, c, part, :],
            send_sem=back_ssem.at[turn, c],
            recv_sem=back_rsem.at[turn, c],
            device_id=(tiles_back[k], off),
            device_id_type=MESH,
        )

    def ahead_copy(turn, c, k):
        return pltpu.make_async_remote_copy(
            src_ref=ahead_send.at[turn, c, pl.ds(k * PART, PART), :],
            dst_ref=slots.at[turn, c, pl.ds(OWN + k * PART, PART), :],
            send_sem=ahead_ssem.at[turn, c],
            recv_sem=ahead_rsem.at[turn, c],
            device_id=(tiles_to[k], off),
            device_id_type=MESH,
        )

    def edge_copy(turn, side):
        step = 1 - 2 * side
        return pltpu.make_async_remote_copy(
            src_ref=edge_send.at[turn, side],
            dst_ref=edge_land.at[turn, side],
            send_sem=edge_ssem.at[turn, side],
            recv_sem=edge_rsem.at[turn, side],
            device_id=(mid, lax.rem(off + step + n_off, n_off)),
            device_id_type=MESH,
        )

    def await_bytes(ref, sem):
        pltpu.make_async_copy(ref, ref, sem).wait()

    def adjoint_chunk(turn, c, values, first=False):
        for p in range(PATTERNS):
            if first and c == 0:
                loads[p].wait()
            part = dot_t(values, moveout[p, cols(c), :])
            spread[p * trace_rows : (p + 1) * trace_rows, :] = part.astype(BF16)
        sums = dot(spread_to[...], spread[...])
        own[c] = sums[:OWN]
        back_send[turn, c] = sums[OWN:].astype(BF16)
        if first and c == 0:
            pl.semaphore_wait(barrier, len(greeted))
        for k in FAR_FIRST:
            back_copy(turn, c, k).start()

    def landed(turn, c):
        await_bytes(back_land.at[turn, c], back_rsem.at[turn, c])
        return own[c] + dot(land_at, back_land[turn, c])

    def ahead_chunk(turn, c, part):
        rounded = part.astype(BF16)
        ahead_send[turn, c] = dot(take_from, rounded).astype(BF16)
        for k in FAR_FIRST:
            ahead_copy(turn, c, k).start()
        slots[turn, c, :OWN, :] = rounded

    def send_edges(turn, field):
        cube = field[...].reshape(CELLS, BINS, samples)
        edge_send[turn, 0] = cube[:, BINS - 1, :]
        edge_send[turn, 1] = cube[:, 0, :]
        for side in range(2):
            edge_copy(turn, side).start()

    def smoothed(turn, field):
        for side in range(2):
            await_bytes(edge_land.at[turn, side], edge_rsem.at[turn, side])
        before = jnp.where(off == 0, 0.0, edge_land[turn, 0])
        after = jnp.where(off == n_off - 1, 0.0, edge_land[turn, 1])
        cube = field[...].reshape(CELLS, BINS, samples)
        padded = jnp.concatenate([before[:, None, :], cube, after[:, None, :]], axis=1)
        out = smooth_weight * (2.0 * cube - padded[:, :-2] - padded[:, 2:])
        return out.reshape(OWN, samples)

    def forward(turn):
        out = jnp.zeros((trace_rows, samples), F32)
        for c in range(CHUNKS):
            await_bytes(slots.at[turn, c, pl.ds(OWN, AWAY), :], ahead_rsem.at[turn, c])
            sums = dot(pick[...], slots[turn, c]).astype(BF16)
            for p in range(PATTERNS):
                out = out + dot(sums[p * trace_rows : (p + 1) * trace_rows], moveout[p, cols(c), :])
        return out

    def total_rows(turn, stage):
        return total_land.at[turn, stage, pl.ds(0, len(stages[stage])), :]

    def total_start(turn, stage, mine):
        total_send[turn, stage, 0:1, :] = mine
        for d, device in enumerate(stages[stage]):
            pltpu.make_async_remote_copy(
                src_ref=total_send.at[turn, stage, pl.ds(0, 1), :],
                dst_ref=total_land.at[turn, stage, pl.ds(d, 1), :],
                send_sem=total_ssem.at[turn, stage],
                recv_sem=total_rsem.at[turn, stage],
                device_id=device,
                device_id_type=MESH,
            ).start()

    def total_end(turn, stage):
        await_bytes(total_rows(turn, stage), total_rsem.at[turn, stage])
        heard = total_land[turn, stage, 0 : len(stages[stage]), :]
        return total_send[turn, stage, 0:1, :] + jnp.sum(heard, axis=0, keepdims=True)

    lane = lax.broadcasted_iota(jnp.int32, (1, 128), 1)

    def packed(parts):
        out = jnp.zeros((1, 128), F32)
        for i, part in enumerate(parts):
            part = part + pltpu.roll(part, 64, 1)
            part = part + pltpu.roll(part, 32, 1)
            out = jnp.where(lane // 32 == i, part, out)
        return out

    def unpacked(row, i):
        return jnp.sum(jnp.where(lane // 32 == i, row, 0.0), axis=1, keepdims=True)

    values = traces_in[...]
    for c in range(CHUNKS):
        adjoint_chunk(0, c, values, first=True)
    heard = values.astype(F32)
    power = by_lanes(heard * heard)
    norm = jnp.zeros((1, 128), F32)
    for c in range(CHUNKS):
        part = landed(0, c)
        ahead_chunk(0, c, part)
        field0[:, cols(c)] = part
        norm = norm + by_lanes(part * part)
    total_start(0, 0, packed((power, norm)))

    send_edges(0, field0)
    smooth[...] = smoothed(0, field0)
    cross = by_lanes(field0[...] * smooth[...])
    values = forward(0).astype(BF16)
    heard = values.astype(F32)
    curve_r = by_lanes(heard * heard) + cross
    adjoint_chunk(1, 0, values)
    total_start(0, 1, total_end(0, 0))
    for c in range(1, CHUNKS):
        adjoint_chunk(1, c, values)
    sums = total_end(0, 1)
    power, rr = unpacked(sums, 0), unpacked(sums, 1)
    usual = jnp.maximum(2.0 * rr / power, 1.0 / 128.0)
    slope = 1.5 * (usual + jnp.minimum(usual, 2.0 * smooth_weight))
    guess = 1.0 / slope
    norm = jnp.zeros((1, 128), F32)
    for c in range(CHUNKS):
        part = field0[:, cols(c)] - guess * (landed(1, c) + smooth[:, cols(c)])
        ahead_chunk(1, c, part)
        field1[:, cols(c)] = part
        norm = norm + by_lanes(part * part)

    send_edges(1, field1)
    smooth[...] = smoothed(1, field1)
    cross = by_lanes(field1[...] * smooth[...])
    values = forward(1).astype(BF16)
    heard = values.astype(F32)
    total_start(1, 0, packed((curve_r, norm, by_lanes(heard * heard) + cross)))
    for c in range(CHUNKS):
        adjoint_chunk(2, c, values)
    total_start(1, 1, total_end(1, 0))
    for c in range(CHUNKS):
        smooth[:, cols(c)] = landed(2, c) + smooth[:, cols(c)]
    sums = total_end(1, 1)
    ra, zz, za = (unpacked(sums, i) for i in range(3))

    step_0 = rr / ra
    t = step_0 * slope
    rest = 1.0 - t
    rz = rr - guess * ra
    norm_1 = rest * (rest * rr + 2.0 * t * rz) + t * (t * zz)
    curve_1 = rest * (rest * ra + 2.0 * t * ((rz - zz) * slope)) + t * (t * za)
    ratio = norm_1 / rr
    step_1 = norm_1 / (curve_1 - ratio * (norm_1 / step_0))
    for c in range(CHUNKS):
        r, z = field0[:, cols(c)], field1[:, cols(c)]
        cube = (CELLS, BINS, width)
        solution_ref[:, :, cols(c)] = ((step_0 + step_1 * (ratio + rest)) * r + (step_1 * t) * z).reshape(cube)
        residual_ref[:, :, cols(c)] = (
            rest * r + t * z - (step_1 * (ratio + rest) * slope) * (r - z) - (step_1 * t) * smooth[:, cols(c)]
        ).reshape(cube)

    for turn in range(3):
        for c in range(CHUNKS):
            await_bytes(back_send.at[turn, c], back_ssem.at[turn, c])
    for turn in range(2):
        for c in range(CHUNKS):
            await_bytes(ahead_send.at[turn, c], ahead_ssem.at[turn, c])
        for side in range(2):
            await_bytes(edge_send.at[turn, side], edge_ssem.at[turn, side])
        for stage in range(2):
            await_bytes(total_rows(turn, stage), total_ssem.at[turn, stage])


def shards(sizes, traces, kernels, send_list, aper_slot, aper_pattern, trace_bin, trace_count):
    n_mid, n_off, n_z = sizes
    n_y = n_mid // n_z
    trace_rows, samples = traces.shape
    width = samples // CHUNKS
    vmem = pl.BlockSpec(memory_space=pltpu.VMEM)
    hbm = pl.BlockSpec(memory_space=pltpu.HBM)
    shape = jax.ShapeDtypeStruct((CELLS, BINS, samples), F32)
    return pl.pallas_call(
        functools.partial(body, sizes),
        out_shape=(shape, shape),
        in_specs=[hbm] * 7,
        out_specs=(vmem, vmem),
        scratch_shapes=[
            pltpu.VMEM((PATTERNS, samples, samples), BF16),
            pltpu.VMEM((trace_rows, samples), BF16),
            pltpu.VMEM(send_list.shape, jnp.int32),
            pltpu.VMEM((APER, trace_rows), jnp.int32),
            pltpu.VMEM((APER, trace_rows), jnp.int32),
            pltpu.VMEM((trace_rows,), jnp.int32),
            pltpu.VMEM((trace_rows,), jnp.int32),
            pltpu.VMEM((PATTERNS * trace_rows, ROWS), BF16),
            pltpu.VMEM((ROWS, PATTERNS * trace_rows), BF16),
            pltpu.VMEM((PATTERNS * trace_rows, width), BF16),
            pltpu.VMEM((CHUNKS, OWN, width), F32),
            pltpu.VMEM((3, CHUNKS, AWAY, width), BF16),
            pltpu.VMEM((3, CHUNKS, AWAY, width), BF16),
            pltpu.VMEM((2, CHUNKS, ROWS, width), BF16),
            pltpu.VMEM((2, CHUNKS, AWAY, width), BF16),
            pltpu.VMEM((OWN, samples), F32),
            pltpu.VMEM((OWN, samples), F32),
            pltpu.VMEM((OWN, samples), F32),
            pltpu.VMEM((2, 2, CELLS, samples), F32),
            pltpu.VMEM((2, 2, CELLS, samples), F32),
            pltpu.VMEM((2, 2, 8, 128), F32),
            pltpu.VMEM((2, 2, max(n_z * 2, n_y * n_off // 2), 128), F32),
            pltpu.SemaphoreType.DMA((PATTERNS,)),
            pltpu.SemaphoreType.DMA((6,)),
            pltpu.SemaphoreType.DMA((3, CHUNKS)),
            pltpu.SemaphoreType.DMA((3, CHUNKS)),
            pltpu.SemaphoreType.DMA((2, CHUNKS)),
            pltpu.SemaphoreType.DMA((2, CHUNKS)),
            pltpu.SemaphoreType.DMA((2, 2)),
            pltpu.SemaphoreType.DMA((2, 2)),
            pltpu.SemaphoreType.DMA((2, 2)),
            pltpu.SemaphoreType.DMA((2, 2)),
        ],
        compiler_params=pltpu.CompilerParams(
            collective_id=0, has_side_effects=True, vmem_limit_bytes=60 * 2**20
        ),
        name="inversion",
    )(traces, kernels, send_list, aper_slot, aper_pattern, trace_bin, trace_count)


def solution(mesh):
    n_mid, n_off = mesh.shape["mid"], mesh.shape["off"]
    n_z = 16 if n_mid % 16 == 0 else 4
    in_specs = (
        P(("mid", "off"), None),
        P(),
        P("mid", None, None),
        P(None, ("mid", "off")),
        P(None, ("mid", "off")),
        P(("mid", "off")),
        P(("mid", "off")),
    )
    out_specs = (P("mid", "off", None), P("mid", "off", None))
    return jax.shard_map(
        functools.partial(shards, (n_mid, n_off, n_z)),
        mesh=mesh,
        in_specs=in_specs,
        out_specs=out_specs,
        check_vma=False,
    )
```

```python
import functools

import jax
import jax.numpy as jnp
from jax import lax
from jax.experimental import pallas as pl
from jax.experimental.pallas import tpu as pltpu
from jax.sharding import PartitionSpec as P

MESH = pl.DeviceIdType.MESH
PATTERNS = 8
APER = 8
CELLS = 8
SEND = 4
DIRS = 4
BINS = 8
OWN = CELLS * BINS
PART = SEND * BINS
AWAY = DIRS * PART
ROWS = OWN + AWAY
CHUNKS = 2
SHIFTS = (1, -1, 2, -2)
FAR_FIRST = (2, 3, 0, 1)
smooth_weight = 2.0
F32 = jnp.float32
BF16 = jnp.bfloat16


def dot(a, b):
    return jnp.dot(a, b, preferred_element_type=F32)


def dot_t(a, b):
    return lax.dot_general(a, b, (((1,), (1,)), ((), ())), preferred_element_type=F32)


def by_lanes(x):
    rows, n = x.shape
    x = x.reshape(rows // 8, 8, n).sum(0)
    x = sum(x[:, i : i + 128] for i in range(0, n, 128))
    return jnp.sum(x, axis=0, keepdims=True)


def body(
    sizes,
    traces_ref,
    kernels_ref,
    send_ref,
    slot_ref,
    pattern_ref,
    bin_ref,
    count_ref,
    first_ref,
    second_ref,
    image_ref,
    weights_ref,
    moveout,
    traces_in,
    send_in,
    slot_in,
    pattern_in,
    bin_in,
    count_in,
    turned,
    pick,
    spread_to,
    spread,
    own,
    back_send,
    back_land,
    slots,
    ahead_send,
    field0,
    field1,
    smooth,
    edge_send,
    edge_land,
    total_send,
    total_land,
    load_sem,
    table_sem,
    store_sem,
    back_ssem,
    back_rsem,
    ahead_ssem,
    ahead_rsem,
    edge_ssem,
    edge_rsem,
    total_ssem,
    total_rsem,
):
    n_mid, n_off, n_z = sizes
    n_y, n_x = n_mid // n_z, n_off // 2
    samples = moveout.shape[2]
    trace_rows = traces_in.shape[0]
    width = samples // CHUNKS
    mid = lax.axis_index("mid")
    off = lax.axis_index("off")
    row_y, col_z = lax.div(mid, n_z), lax.rem(mid, n_z)
    col_x, core = lax.div(off, 2), lax.rem(off, 2)

    def tile_at(shift):
        return lax.rem(mid + (shift + n_mid), n_mid)

    tiles_to = [tile_at(s) for s in SHIFTS]
    tiles_back = [tile_at(-s) for s in SHIFTS]

    def farthest_first(sizes_2, where):
        pairs = [(i, j) for i in range(sizes_2[0]) for j in range(sizes_2[1]) if i or j]
        pairs.sort(key=lambda ij: -min(ij[0], sizes_2[0] - ij[0]) - min(ij[1], sizes_2[1] - ij[1]))
        return [where(i, j) for i, j in pairs]

    line = farthest_first(
        (n_z, 2), lambda i, j: (row_y * n_z + lax.rem(col_z + i, n_z), col_x * 2 + lax.rem(core + j, 2))
    )
    plane = farthest_first(
        (n_y, n_x),
        lambda i, j: (lax.rem(row_y + i, n_y) * n_z + col_z, lax.rem(col_x + j, n_x) * 2 + core),
    )
    stages = (plane, line)

    tables = [
        pltpu.make_async_copy(src, dst, table_sem.at[i])
        for i, (src, dst) in enumerate(
            (
                (slot_ref, slot_in),
                (pattern_ref, pattern_in),
                (bin_ref, bin_in),
                (count_ref, count_in),
                (send_ref, send_in),
                (traces_ref, traces_in),
            )
        )
    ]
    for load in tables:
        load.start()
    loads = [
        pltpu.make_async_copy(kernels_ref.at[p], moveout.at[p], load_sem.at[p]) for p in range(PATTERNS)
    ]
    for load in loads:
        load.start()

    barrier = pltpu.get_barrier_semaphore()
    greeted = [device for stage in stages for device in stage]
    greeted += [(tile, off) for tile in tiles_to]
    greeted += [(mid, lax.rem(off + 1, n_off)), (mid, lax.rem(off + n_off - 1, n_off))]
    for device in greeted:
        pl.semaphore_signal(barrier, inc=1, device_id=device, device_id_type=MESH)
    for load in tables:
        load.wait()

    slot = slot_in[...]
    live = lax.broadcasted_iota(jnp.int32, slot.shape, 0) < count_in[...].reshape(1, trace_rows)
    for k in range(DIRS):
        source = mid - SHIFTS[k]
        here = (source >= 0) & (source < n_mid)
        inside = (slot >= CELLS + k * SEND) & (slot < CELLS + (k + 1) * SEND)
        live = live & (jnp.logical_not(inside) | here)
    code = pattern_in[...] * ROWS + slot * BINS + bin_in[...].reshape(1, trace_rows)
    code = jnp.where(live, code, -1)
    row_id = lax.broadcasted_iota(jnp.int32, (ROWS, trace_rows), 0)
    for p in range(PATTERNS):
        count = jnp.zeros((ROWS, trace_rows), F32)
        for j in range(APER):
            count = count + jnp.where(code[j : j + 1, :] - p * ROWS == row_id, 1.0, 0.0)
        spread_to[:, p * trace_rows : (p + 1) * trace_rows] = count.astype(BF16)
        pick[p * trace_rows : (p + 1) * trace_rows, :] = count.T.astype(BF16)

    entry = lax.broadcasted_iota(jnp.int32, (OWN, AWAY), 1)
    listed = jnp.zeros((OWN, AWAY), jnp.int32)
    for k in range(DIRS):
        for m in range(SEND):
            listed = jnp.where(entry // BINS == k * SEND + m, send_in[0, k : k + 1, m : m + 1], listed)
    place = listed * BINS + entry % BINS
    land_f32 = jnp.where(place == lax.broadcasted_iota(jnp.int32, (OWN, AWAY), 0), 1.0, 0.0)
    land_at = land_f32.astype(BF16)
    take_from = land_f32.T.astype(BF16)

    def cols(c):
        return slice(c * width, (c + 1) * width)

    def back_copy(turn, c, k):
        part = pl.ds(k * PART, PART)
        return pltpu.make_async_remote_copy(
            src_ref=back_send.at[turn, c, part, :],
            dst_ref=back_land.at[turn, c, part, :],
            send_sem=back_ssem.at[turn, c],
            recv_sem=back_rsem.at[turn, c],
            device_id=(tiles_back[k], off),
            device_id_type=MESH,
        )

    def ahead_copy(turn, c, k):
        return pltpu.make_async_remote_copy(
            src_ref=ahead_send.at[turn, c, pl.ds(k * PART, PART), :],
            dst_ref=slots.at[turn, c, pl.ds(OWN + k * PART, PART), :],
            send_sem=ahead_ssem.at[turn, c],
            recv_sem=ahead_rsem.at[turn, c],
            device_id=(tiles_to[k], off),
            device_id_type=MESH,
        )

    def edge_copy(turn, side):
        step = 1 - 2 * side
        return pltpu.make_async_remote_copy(
            src_ref=edge_send.at[turn, side],
            dst_ref=edge_land.at[turn, side],
            send_sem=edge_ssem.at[turn, side],
            recv_sem=edge_rsem.at[turn, side],
            device_id=(mid, lax.rem(off + step + n_off, n_off)),
            device_id_type=MESH,
        )

    def await_bytes(ref, sem):
        pltpu.make_async_copy(ref, ref, sem).wait()

    def adjoint_chunk(turn, c, values, first=False):
        groups = 2 if first else 1
        each = PATTERNS // groups
        for g in range(groups):
            if first:
                if c == 0:
                    for load in loads[g * each : (g + 1) * each]:
                        load.wait()
                wide = dot_t(values, moveout[g * each : (g + 1) * each, cols(c), :].reshape(each * width, samples))
            else:
                wide = dot(values, turned[c])
            wide = wide.astype(BF16)
            for i in range(each):
                p = g * each + i
                spread[p * trace_rows : (p + 1) * trace_rows, :] = wide[:, i * width : (i + 1) * width]
        sums = dot(spread_to[...], spread[...])
        own[c] = sums[:OWN]
        back_send[turn, c] = sums[OWN:].astype(BF16)
        if first and c == 0:
            pl.semaphore_wait(barrier, len(greeted))
        for k in FAR_FIRST:
            back_copy(turn, c, k).start()
        return sums

    def landed(turn, c):
        await_bytes(back_land.at[turn, c], back_rsem.at[turn, c])
        return own[c] + dot(land_at, back_land[turn, c])

    def ahead_chunk(turn, c, part, field):
        rounded = part.astype(BF16)
        ahead_send[turn, c] = dot(take_from, rounded).astype(BF16)
        for k in FAR_FIRST:
            ahead_copy(turn, c, k).start()
        slots[turn, c, :OWN, :] = rounded
        field[:, cols(c)] = part

    def send_edges(turn, field):
        cube = field[...].reshape(CELLS, BINS, samples)
        edge_send[turn, 0] = cube[:, BINS - 1, :]
        edge_send[turn, 1] = cube[:, 0, :]
        for side in range(2):
            edge_copy(turn, side).start()

    def smoothed(turn, field):
        for side in range(2):
            await_bytes(edge_land.at[turn, side], edge_rsem.at[turn, side])
        before = jnp.where(off == 0, 0.0, edge_land[turn, 0])
        after = jnp.where(off == n_off - 1, 0.0, edge_land[turn, 1])
        cube = field[...].reshape(CELLS, BINS, samples)
        padded = jnp.concatenate([before[:, None, :], cube, after[:, None, :]], axis=1)
        out = smooth_weight * (2.0 * cube - padded[:, :-2] - padded[:, 2:])
        return out.reshape(OWN, samples)

    def forward(turn):
        out = None
        for c in range(CHUNKS):
            await_bytes(slots.at[turn, c, pl.ds(OWN, AWAY), :], ahead_rsem.at[turn, c])
            sums = dot(pick[...], slots[turn, c]).astype(BF16)
            wide = jnp.concatenate([sums[p * trace_rows : (p + 1) * trace_rows] for p in range(PATTERNS)], axis=1)
            part = dot(wide, moveout[:, cols(c), :].reshape(PATTERNS * width, samples))
            out = part if out is None else out + part
        return out

    def total_rows(turn, stage):
        return total_land.at[turn, stage, pl.ds(0, len(stages[stage])), :]

    def total_start(turn, stage, mine):
        total_send[turn, stage, 0:1, :] = mine
        for d, device in enumerate(stages[stage]):
            pltpu.make_async_remote_copy(
                src_ref=total_send.at[turn, stage, pl.ds(0, 1), :],
                dst_ref=total_land.at[turn, stage, pl.ds(d, 1), :],
                send_sem=total_ssem.at[turn, stage],
                recv_sem=total_rsem.at[turn, stage],
                device_id=device,
                device_id_type=MESH,
            ).start()

    def total_end(turn, stage):
        await_bytes(total_rows(turn, stage), total_rsem.at[turn, stage])
        heard = total_land[turn, stage, 0 : len(stages[stage]), :]
        return total_send[turn, stage, 0:1, :] + jnp.sum(heard, axis=0, keepdims=True)

    lane = lax.broadcasted_iota(jnp.int32, (1, 128), 1)

    def packed(parts):
        out = jnp.zeros((1, 128), F32)
        for i, part in enumerate(parts):
            part = part + pltpu.roll(part, 64, 1)
            part = part + pltpu.roll(part, 32, 1)
            out = jnp.where(lane // 32 == i, part, out)
        return out

    def unpacked(row, i):
        return jnp.sum(jnp.where(lane // 32 == i, row, 0.0), axis=1, keepdims=True)

    stores = [
        pltpu.make_async_copy(src, dst, store_sem.at[i])
        for i, (src, dst) in enumerate(((field0, first_ref), (field1, second_ref), (smooth, image_ref)))
    ]

    values = traces_in[...]
    local = jnp.zeros((1, 128), F32)
    for c in range(CHUNKS):
        part = adjoint_chunk(0, c, values, first=True)
        local = local + by_lanes(part * part)
    heard = values.astype(F32)
    total_start(0, 0, packed((by_lanes(heard * heard), local)))
    for c in range(CHUNKS):
        for p in range(PATTERNS):
            turned[c, :, p * width : (p + 1) * width] = moveout[p, cols(c), :].T
    norm = jnp.zeros((1, 128), F32)
    for c in range(CHUNKS):
        part = landed(0, c)
        ahead_chunk(0, c, part, field0)
        norm = norm + by_lanes(part * part)
    norm_r = norm

    send_edges(0, field0)
    stores[0].start()
    total_start(0, 1, total_end(0, 0))
    smooth[...] = smoothed(0, field0)
    cross = by_lanes(field0[...] * smooth[...])
    values = forward(0).astype(BF16)
    heard = values.astype(F32)
    curve_r = by_lanes(heard * heard) + cross
    for c in range(CHUNKS):
        adjoint_chunk(1, c, values)
    sums = total_end(0, 1)
    usual = jnp.maximum(2.0 * unpacked(sums, 1) / unpacked(sums, 0), 1.0 / 128.0)
    slope = 1.5 * (usual + jnp.minimum(usual, 2.0 * smooth_weight))
    guess = 1.0 / slope
    norm = jnp.zeros((1, 128), F32)
    for c in range(CHUNKS):
        part = field0[:, cols(c)] - guess * (landed(1, c) + smooth[:, cols(c)])
        ahead_chunk(1, c, part, field1)
        norm = norm + by_lanes(part * part)

    send_edges(1, field1)
    stores[1].start()
    smooth[...] = smoothed(1, field1)
    cross = by_lanes(field1[...] * smooth[...])
    values = forward(1).astype(BF16)
    heard = values.astype(F32)
    total_start(1, 0, packed((curve_r, norm, norm_r, by_lanes(heard * heard) + cross)))
    for c in range(CHUNKS):
        adjoint_chunk(2, c, values)
    total_start(1, 1, total_end(1, 0))
    for c in range(CHUNKS):
        smooth[:, cols(c)] = landed(2, c) + smooth[:, cols(c)]
    stores[2].start()
    sums = total_end(1, 1)
    ra, zz, rr, za = (unpacked(sums, i) for i in range(4))

    step_0 = rr / ra
    t = step_0 * slope
    rest = 1.0 - t
    rz = rr - guess * ra
    norm_1 = rest * (rest * rr + 2.0 * t * rz) + t * (t * zz)
    curve_1 = rest * (rest * ra + 2.0 * t * ((rz - zz) * slope)) + t * (t * za)
    ratio = norm_1 / rr
    step_1 = norm_1 / (curve_1 - ratio * (norm_1 / step_0))
    along = step_1 * (ratio + rest)
    row = lax.broadcasted_iota(jnp.int32, (8, 128), 0)
    weights = jnp.zeros((8, 128), F32)
    for i, weight in enumerate(
        (step_0 + along, step_1 * t, rest - along * slope, t + along * slope, -(step_1 * t))
    ):
        weights = jnp.where(row == i, weight, weights)
    weights_ref[...] = weights
    for store in stores:
        store.wait()

    for turn in range(3):
        for c in range(CHUNKS):
            await_bytes(back_send.at[turn, c], back_ssem.at[turn, c])
    for turn in range(2):
        for c in range(CHUNKS):
            await_bytes(ahead_send.at[turn, c], ahead_ssem.at[turn, c])
        for side in range(2):
            await_bytes(edge_send.at[turn, side], edge_ssem.at[turn, side])
        for stage in range(2):
            await_bytes(total_rows(turn, stage), total_ssem.at[turn, stage])


def combine(r_ref, z_ref, image_ref, weights_ref, solution_ref, residual_ref):
    weight = [weights_ref[i : i + 1, 0:1] for i in range(5)]
    r, z = r_ref[...], z_ref[...]
    solution_ref[...] = (weight[0] * r + weight[1] * z).reshape(solution_ref.shape)
    left = weight[2] * r + weight[3] * z + weight[4] * image_ref[...]
    residual_ref[...] = left.reshape(residual_ref.shape)


def shards(sizes, traces, kernels, send_list, aper_slot, aper_pattern, trace_bin, trace_count):
    n_mid, n_off, n_z = sizes
    n_y = n_mid // n_z
    trace_rows, samples = traces.shape
    width = samples // CHUNKS
    vmem = pl.BlockSpec(memory_space=pltpu.VMEM)
    hbm = pl.BlockSpec(memory_space=pltpu.HBM)
    field = jax.ShapeDtypeStruct((OWN, samples), F32)
    r, z, image, weights = pl.pallas_call(
        functools.partial(body, sizes),
        out_shape=(field, field, field, jax.ShapeDtypeStruct((8, 128), F32)),
        in_specs=[hbm] * 7,
        out_specs=(hbm, hbm, hbm, vmem),
        scratch_shapes=[
            pltpu.VMEM((PATTERNS, samples, samples), BF16),
            pltpu.VMEM((trace_rows, samples), BF16),
            pltpu.VMEM(send_list.shape, jnp.int32),
            pltpu.VMEM((APER, trace_rows), jnp.int32),
            pltpu.VMEM((APER, trace_rows), jnp.int32),
            pltpu.VMEM((trace_rows,), jnp.int32),
            pltpu.VMEM((trace_rows,), jnp.int32),
            pltpu.VMEM((CHUNKS, samples, PATTERNS * width), BF16),
            pltpu.VMEM((PATTERNS * trace_rows, ROWS), BF16),
            pltpu.VMEM((ROWS, PATTERNS * trace_rows), BF16),
            pltpu.VMEM((PATTERNS * trace_rows, width), BF16),
            pltpu.VMEM((CHUNKS, OWN, width), F32),
            pltpu.VMEM((3, CHUNKS, AWAY, width), BF16),
            pltpu.VMEM((3, CHUNKS, AWAY, width), BF16),
            pltpu.VMEM((2, CHUNKS, ROWS, width), BF16),
            pltpu.VMEM((2, CHUNKS, AWAY, width), BF16),
            pltpu.VMEM((OWN, samples), F32),
            pltpu.VMEM((OWN, samples), F32),
            pltpu.VMEM((OWN, samples), F32),
            pltpu.VMEM((2, 2, CELLS, samples), F32),
            pltpu.VMEM((2, 2, CELLS, samples), F32),
            pltpu.VMEM((2, 2, 8, 128), F32),
            pltpu.VMEM((2, 2, max(n_z * 2, n_y * n_off // 2), 128), F32),
            pltpu.SemaphoreType.DMA((PATTERNS,)),
            pltpu.SemaphoreType.DMA((6,)),
            pltpu.SemaphoreType.DMA((3,)),
            pltpu.SemaphoreType.DMA((3, CHUNKS)),
            pltpu.SemaphoreType.DMA((3, CHUNKS)),
            pltpu.SemaphoreType.DMA((2, CHUNKS)),
            pltpu.SemaphoreType.DMA((2, CHUNKS)),
            pltpu.SemaphoreType.DMA((2, 2)),
            pltpu.SemaphoreType.DMA((2, 2)),
            pltpu.SemaphoreType.DMA((2, 2)),
            pltpu.SemaphoreType.DMA((2, 2)),
        ],
        compiler_params=pltpu.CompilerParams(
            collective_id=0, has_side_effects=True, vmem_limit_bytes=60 * 2**20
        ),
        name="inversion",
    )(traces, kernels, send_list, aper_slot, aper_pattern, trace_bin, trace_count)
    shape = jax.ShapeDtypeStruct((CELLS, BINS, samples), F32)
    return pl.pallas_call(
        combine,
        out_shape=(shape, shape),
        in_specs=[vmem] * 4,
        out_specs=(vmem, vmem),
        compiler_params=pltpu.CompilerParams(vmem_limit_bytes=60 * 2**20),
        name="combine",
    )(r, z, image, weights)


def solution(mesh):
    n_mid, n_off = mesh.shape["mid"], mesh.shape["off"]
    n_z = 16 if n_mid % 16 == 0 else 4
    in_specs = (
        P(("mid", "off"), None),
        P(),
        P("mid", None, None),
        P(None, ("mid", "off")),
        P(None, ("mid", "off")),
        P(("mid", "off")),
        P(("mid", "off")),
    )
    out_specs = (P("mid", "off", None), P("mid", "off", None))
    return jax.shard_map(
        functools.partial(shards, (n_mid, n_off, n_z)),
        mesh=mesh,
        in_specs=in_specs,
        out_specs=out_specs,
        check_vma=False,
    )
```

```python
import functools

import jax
import jax.numpy as jnp
from jax import lax
from jax.experimental import pallas as pl
from jax.experimental.pallas import tpu as pltpu
from jax.sharding import PartitionSpec as P

MESH = pl.DeviceIdType.MESH
PATTERNS = 8
APER = 8
CELLS = 8
SEND = 4
DIRS = 4
BINS = 8
OWN = CELLS * BINS
PART = SEND * BINS
AWAY = DIRS * PART
ROWS = OWN + AWAY
CHUNKS = 2
SHIFTS = (1, -1, 2, -2)
FAR_FIRST = (2, 3, 0, 1)
SHRINK = 2.0 ** -14
smooth_weight = 2.0
F32 = jnp.float32
BF16 = jnp.bfloat16


def dot(a, b):
    return jnp.dot(a, b, preferred_element_type=F32)


def dot_t(a, b):
    return lax.dot_general(a, b, (((1,), (1,)), ((), ())), preferred_element_type=F32)


def by_lanes(x):
    rows, n = x.shape
    x = x.reshape(rows // 8, 8, n).sum(0)
    x = sum(x[:, i : i + 128] for i in range(0, n, 128))
    return jnp.sum(x, axis=0, keepdims=True)


def body(
    sizes,
    traces_ref,
    kernels_ref,
    send_ref,
    slot_ref,
    pattern_ref,
    bin_ref,
    count_ref,
    first_ref,
    second_ref,
    image_ref,
    weights_ref,
    moveout,
    traces_in,
    send_in,
    slot_in,
    pattern_in,
    bin_in,
    count_in,
    turned,
    pick,
    spread_to,
    spread,
    spread_low,
    own,
    back_send,
    back_land,
    fine_send,
    fine_land,
    slots,
    ahead_send,
    field0,
    field1,
    smooth,
    edge_send,
    edge_land,
    total_send,
    total_land,
    load_sem,
    table_sem,
    store_sem,
    back_ssem,
    back_rsem,
    ahead_ssem,
    ahead_rsem,
    edge_ssem,
    edge_rsem,
    total_ssem,
    total_rsem,
    meet_sem,
):
    n_mid, n_off, n_z = sizes
    n_y, n_x = n_mid // n_z, n_off // 2
    samples = moveout.shape[2]
    trace_rows = traces_in.shape[0]
    width = samples // CHUNKS
    mid = lax.axis_index("mid")
    off = lax.axis_index("off")
    row_y, col_z = lax.div(mid, n_z), lax.rem(mid, n_z)
    col_x, core = lax.div(off, 2), lax.rem(off, 2)

    def tile_at(shift):
        return lax.rem(mid + (shift + n_mid), n_mid)

    tiles_to = [tile_at(s) for s in SHIFTS]
    tiles_back = [tile_at(-s) for s in SHIFTS]

    def farthest_first(sizes_2, where):
        pairs = [(i, j) for i in range(sizes_2[0]) for j in range(sizes_2[1]) if i or j]
        pairs.sort(key=lambda ij: -min(ij[0], sizes_2[0] - ij[0]) - min(ij[1], sizes_2[1] - ij[1]))
        return [where(i, j) for i, j in pairs]

    line = farthest_first(
        (n_z, 2), lambda i, j: (row_y * n_z + lax.rem(col_z + i, n_z), col_x * 2 + lax.rem(core + j, 2))
    )
    plane = farthest_first(
        (n_y, n_x),
        lambda i, j: (lax.rem(row_y + i, n_y) * n_z + col_z, lax.rem(col_x + j, n_x) * 2 + core),
    )
    stages = (plane, line)

    tables = [
        pltpu.make_async_copy(src, dst, table_sem.at[i])
        for i, (src, dst) in enumerate(
            (
                (slot_ref, slot_in),
                (pattern_ref, pattern_in),
                (bin_ref, bin_in),
                (count_ref, count_in),
                (send_ref, send_in),
                (traces_ref, traces_in),
            )
        )
    ]
    loads = [
        pltpu.make_async_copy(kernels_ref.at[p], moveout.at[p], load_sem.at[p]) for p in range(PATTERNS)
    ]

    barrier = pltpu.get_barrier_semaphore()

    def greet(devices):
        for device in devices:
            pl.semaphore_signal(barrier, inc=1, device_id=device, device_id_type=MESH)

    def around(count, steps):
        return sorted({d % count for step in steps for d in (step, -step)} - {0})

    def at_z(steps):
        return [(row_y * n_z + lax.rem(col_z + d, n_z), off) for d in around(n_z, steps)]

    def at_y(steps):
        return [(lax.rem(row_y + d, n_y) * n_z + col_z, off) for d in around(n_y, steps)]

    def at_x(steps):
        return [(mid, lax.rem(col_x + d, n_x) * 2 + core) for d in around(n_x, steps)]

    partner = [(mid, col_x * 2 + 1 - core)]
    near = [(tile, off) for tile in tiles_to]
    near += [(mid, lax.rem(off + 1, n_off)), (mid, lax.rem(off + n_off - 1, n_off))]
    near += at_z((1, 2)) + at_y((1,)) + at_x((1,)) + partner
    rounds = (at_z((2,)) + at_y((1,)) + at_x((1,)), at_z((4,)) + at_y((2,)), at_x((1, 2)) + partner)

    def meet(i):
        for device in rounds[i]:
            pl.semaphore_signal(meet_sem.at[i], inc=1, device_id=device, device_id_type=MESH)

    def met(i):
        if rounds[i]:
            pl.semaphore_wait(meet_sem.at[i], len(rounds[i]))

    greet(near)
    for load in tables + loads:
        load.start()
    for load in tables:
        load.wait()

    slot = slot_in[...]
    live = lax.broadcasted_iota(jnp.int32, slot.shape, 0) < count_in[...].reshape(1, trace_rows)
    for k in range(DIRS):
        source = mid - SHIFTS[k]
        here = (source >= 0) & (source < n_mid)
        inside = (slot >= CELLS + k * SEND) & (slot < CELLS + (k + 1) * SEND)
        live = live & (jnp.logical_not(inside) | here)
    code = pattern_in[...] * ROWS + slot * BINS + bin_in[...].reshape(1, trace_rows)
    code = jnp.where(live, code, -1)
    row_id = lax.broadcasted_iota(jnp.int32, (ROWS, trace_rows), 0)
    for p in range(PATTERNS):
        count = jnp.zeros((ROWS, trace_rows), F32)
        for j in range(APER):
            count = count + jnp.where(code[j : j + 1, :] - p * ROWS == row_id, 1.0, 0.0)
        spread_to[:, p * trace_rows : (p + 1) * trace_rows] = count.astype(BF16)
        pick[p * trace_rows : (p + 1) * trace_rows, :] = count.T.astype(BF16)

    entry = lax.broadcasted_iota(jnp.int32, (OWN, AWAY), 1)
    listed = jnp.zeros((OWN, AWAY), jnp.int32)
    for k in range(DIRS):
        for m in range(SEND):
            listed = jnp.where(entry // BINS == k * SEND + m, send_in[0, k : k + 1, m : m + 1], listed)
    place = listed * BINS + entry % BINS
    land_f32 = jnp.where(place == lax.broadcasted_iota(jnp.int32, (OWN, AWAY), 0), 1.0, 0.0)
    land_at = land_f32.astype(BF16)
    take_from = land_f32.T.astype(BF16)

    def cols(c):
        return slice(c * width, (c + 1) * width)

    def back_copy(turn, c, k):
        part = pl.ds(k * PART, PART)
        return pltpu.make_async_remote_copy(
            src_ref=back_send.at[turn, c, part, :],
            dst_ref=back_land.at[turn, c, part, :],
            send_sem=back_ssem.at[turn, c],
            recv_sem=back_rsem.at[turn, c],
            device_id=(tiles_back[k], off),
            device_id_type=MESH,
        )

    def ahead_copy(turn, c, k):
        return pltpu.make_async_remote_copy(
            src_ref=ahead_send.at[turn, c, pl.ds(k * PART, PART), :],
            dst_ref=slots.at[turn, c, pl.ds(OWN + k * PART, PART), :],
            send_sem=ahead_ssem.at[turn, c],
            recv_sem=ahead_rsem.at[turn, c],
            device_id=(tiles_to[k], off),
            device_id_type=MESH,
        )

    def edge_copy(turn, side):
        step = 1 - 2 * side
        return pltpu.make_async_remote_copy(
            src_ref=edge_send.at[turn, side],
            dst_ref=edge_land.at[turn, side],
            send_sem=edge_ssem.at[turn, side],
            recv_sem=edge_rsem.at[turn, side],
            device_id=(mid, lax.rem(off + step + n_off, n_off)),
            device_id_type=MESH,
        )

    def await_bytes(ref, sem):
        pltpu.make_async_copy(ref, ref, sem).wait()

    def adjoint_chunk(turn, c, values, first=False):
        groups = 2 if first else 1
        each = PATTERNS // groups
        for g in range(groups):
            if first:
                if c == 0:
                    for load in loads[g * each : (g + 1) * each]:
                        load.wait()
                wide = dot_t(values, moveout[g * each : (g + 1) * each, cols(c), :].reshape(each * width, samples))
            else:
                wide = dot(values, turned[c])
            wide = wide.astype(BF16)
            for i in range(each):
                p = g * each + i
                spread[p * trace_rows : (p + 1) * trace_rows, :] = wide[:, i * width : (i + 1) * width]
        sums = dot(spread_to[...], spread[...])
        own[c] = sums[:OWN]
        back_send[turn, c] = sums[OWN:].astype(BF16)
        if first and c == 0:
            pl.semaphore_wait(barrier, len(near))
        for k in FAR_FIRST:
            back_copy(turn, c, k).start()
        return sums

    def halves(x):
        high = x.astype(BF16)
        return high, (x - high.astype(F32)).astype(BF16)

    def fine_copy(c, k):
        part = pl.ds(k * PART, PART)
        return pltpu.make_async_remote_copy(
            src_ref=fine_send.at[c, part, :],
            dst_ref=fine_land.at[c, part, :],
            send_sem=back_ssem.at[2, c],
            recv_sem=back_rsem.at[2, c],
            device_id=(tiles_back[k], off),
            device_id_type=MESH,
        )

    def fine_chunk(c, values):
        high, low = halves(values)
        wide = halves(dot(high, turned[c]) + dot(low, turned[c]))
        for p in range(PATTERNS):
            rows = slice(p * trace_rows, (p + 1) * trace_rows)
            for part, to in zip(wide, (spread, spread_low)):
                to[rows, :] = part[:, p * width : (p + 1) * width]
        sums = dot(spread_to[...], spread[...]) + dot(spread_to[...], spread_low[...])
        own[c] = sums[:OWN]
        fine_send[c] = sums[OWN:]
        for k in FAR_FIRST:
            fine_copy(c, k).start()

    def fine_landed(c):
        await_bytes(fine_land.at[c], back_rsem.at[2, c])
        high, low = halves(fine_land[c])
        return own[c] + (dot(land_at, high) + dot(land_at, low))

    def landed(turn, c):
        await_bytes(back_land.at[turn, c], back_rsem.at[turn, c])
        return own[c] + dot(land_at, back_land[turn, c])

    def ahead_chunk(turn, c, part, field):
        rounded = part.astype(BF16)
        ahead_send[turn, c] = dot(take_from, rounded).astype(BF16)
        for k in FAR_FIRST:
            ahead_copy(turn, c, k).start()
        slots[turn, c, :OWN, :] = rounded
        field[:, cols(c)] = part

    def send_edges(turn, field):
        cube = field[...].reshape(CELLS, BINS, samples)
        edge_send[turn, 0] = cube[:, BINS - 1, :]
        edge_send[turn, 1] = cube[:, 0, :]
        for side in range(2):
            edge_copy(turn, side).start()

    def smoothed(turn, field):
        for side in range(2):
            await_bytes(edge_land.at[turn, side], edge_rsem.at[turn, side])
        before = jnp.where(off == 0, 0.0, edge_land[turn, 0])
        after = jnp.where(off == n_off - 1, 0.0, edge_land[turn, 1])
        cube = field[...].reshape(CELLS, BINS, samples)
        padded = jnp.concatenate([before[:, None, :], cube, after[:, None, :]], axis=1)
        out = smooth_weight * (2.0 * cube - padded[:, :-2] - padded[:, 2:])
        return out.reshape(OWN, samples)

    def forward(turn):
        out = None
        for c in range(CHUNKS):
            await_bytes(slots.at[turn, c, pl.ds(OWN, AWAY), :], ahead_rsem.at[turn, c])
            sums = dot(pick[...], slots[turn, c]).astype(BF16)
            wide = jnp.concatenate([sums[p * trace_rows : (p + 1) * trace_rows] for p in range(PATTERNS)], axis=1)
            part = dot(wide, moveout[:, cols(c), :].reshape(PATTERNS * width, samples))
            out = part if out is None else out + part
        return out

    def total_rows(turn, stage):
        return total_land.at[turn, stage, pl.ds(0, len(stages[stage])), :]

    def total_start(turn, stage, mine):
        total_send[turn, stage, 0:1, :] = mine
        for d, device in enumerate(stages[stage]):
            pltpu.make_async_remote_copy(
                src_ref=total_send.at[turn, stage, pl.ds(0, 1), :],
                dst_ref=total_land.at[turn, stage, pl.ds(d, 1), :],
                send_sem=total_ssem.at[turn, stage],
                recv_sem=total_rsem.at[turn, stage],
                device_id=device,
                device_id_type=MESH,
            ).start()

    def total_end(turn, stage):
        await_bytes(total_rows(turn, stage), total_rsem.at[turn, stage])
        heard = total_land[turn, stage, 0 : len(stages[stage]), :]
        return total_send[turn, stage, 0:1, :] + jnp.sum(heard, axis=0, keepdims=True)

    lane = lax.broadcasted_iota(jnp.int32, (1, 128), 1)

    def packed(parts):
        out = jnp.zeros((1, 128), F32)
        for i, part in enumerate(parts):
            part = part + pltpu.roll(part, 64, 1)
            part = part + pltpu.roll(part, 32, 1)
            out = jnp.where(lane // 32 == i, part, out)
        return out

    def unpacked(row, i):
        return jnp.sum(jnp.where(lane // 32 == i, row, 0.0), axis=1, keepdims=True)

    stores = [
        pltpu.make_async_copy(src, dst, store_sem.at[i])
        for i, (src, dst) in enumerate(((field0, first_ref), (field1, second_ref), (smooth, image_ref)))
    ]

    values = traces_in[...]
    for c in range(CHUNKS):
        adjoint_chunk(0, c, values, first=True)
    meet(0)
    for c in range(CHUNKS):
        for p in range(PATTERNS):
            turned[c, :, p * width : (p + 1) * width] = moveout[p, cols(c), :].T
    met(0)
    meet(1)
    norm = jnp.zeros((1, 128), F32)
    for c in range(CHUNKS):
        part = landed(0, c)
        ahead_chunk(0, c, part, field0)
        norm = norm + by_lanes(part * part)
    norm_r = norm

    send_edges(0, field0)
    stores[0].start()
    smooth[...] = smoothed(0, field0)
    cross = by_lanes(field0[...] * smooth[...])
    met(1)
    meet(2)
    values = forward(0).astype(BF16)
    heard = values.astype(F32)
    curve_r = by_lanes(heard * heard) + cross
    for c in range(CHUNKS):
        adjoint_chunk(1, c, values)
    norm = jnp.zeros((1, 128), F32)
    for c in range(CHUNKS):
        part = (landed(1, c) + smooth[:, cols(c)]) * SHRINK
        ahead_chunk(1, c, part, field1)
        norm = norm + by_lanes(part * part)

    send_edges(1, field1)
    stores[1].start()
    smooth[...] = smoothed(1, field1)
    cross = by_lanes(field1[...] * smooth[...])
    met(2)
    heard = forward(1)
    total_start(1, 0, packed((curve_r, norm, norm_r, by_lanes(heard * heard) + cross)))
    for c in range(CHUNKS):
        fine_chunk(c, heard)
    total_start(1, 1, total_end(1, 0))
    for c in range(CHUNKS):
        smooth[:, cols(c)] = fine_landed(c) + smooth[:, cols(c)]
    stores[2].start()
    sums = total_end(1, 1)
    ra, zz, rr, za = (unpacked(sums, i) for i in range(4))

    grow = 1.0 / SHRINK
    step_0, one_over = rr / ra, 1.0 / rr
    scaled = step_0 * grow
    norm_1 = scaled * (scaled * zz) - rr
    more = 1.0 + norm_1 * one_over
    curve_1 = more * (more * ra) - 2.0 * more * (scaled * (zz * grow)) + scaled * (scaled * za)
    step_1 = norm_1 / curve_1
    along = step_1 * more
    row = lax.broadcasted_iota(jnp.int32, (8, 128), 0)
    weights = jnp.zeros((8, 128), F32)
    for i, weight in enumerate(
        (step_0 + along, -(step_1 * scaled), jnp.ones_like(rr), -(scaled + along * grow), step_1 * scaled)
    ):
        weights = jnp.where(row == i, weight, weights)
    weights_ref[...] = weights
    for store in stores:
        store.wait()

    for c in range(CHUNKS):
        for turn in range(2):
            await_bytes(back_send.at[turn, c], back_ssem.at[turn, c])
            await_bytes(ahead_send.at[turn, c], ahead_ssem.at[turn, c])
        await_bytes(fine_send.at[c], back_ssem.at[2, c])
    for turn in range(2):
        for side in range(2):
            await_bytes(edge_send.at[turn, side], edge_ssem.at[turn, side])
    for stage in range(2):
        await_bytes(total_rows(1, stage), total_ssem.at[1, stage])


def combine(r_ref, z_ref, image_ref, weights_ref, solution_ref, residual_ref):
    weight = [weights_ref[i : i + 1, 0:1] for i in range(5)]
    r, z = r_ref[...], z_ref[...]
    solution_ref[...] = (weight[0] * r + weight[1] * z).reshape(solution_ref.shape)
    left = weight[2] * r + weight[3] * z + weight[4] * image_ref[...]
    residual_ref[...] = left.reshape(residual_ref.shape)


def shards(sizes, traces, kernels, send_list, aper_slot, aper_pattern, trace_bin, trace_count):
    n_mid, n_off, n_z = sizes
    n_y = n_mid // n_z
    trace_rows, samples = traces.shape
    width = samples // CHUNKS
    vmem = pl.BlockSpec(memory_space=pltpu.VMEM)
    hbm = pl.BlockSpec(memory_space=pltpu.HBM)
    field = jax.ShapeDtypeStruct((OWN, samples), F32)
    r, z, image, weights = pl.pallas_call(
        functools.partial(body, sizes),
        out_shape=(field, field, field, jax.ShapeDtypeStruct((8, 128), F32)),
        in_specs=[hbm] * 7,
        out_specs=(hbm, hbm, hbm, vmem),
        scratch_shapes=[
            pltpu.VMEM((PATTERNS, samples, samples), BF16),
            pltpu.VMEM((trace_rows, samples), BF16),
            pltpu.VMEM(send_list.shape, jnp.int32),
            pltpu.VMEM((APER, trace_rows), jnp.int32),
            pltpu.VMEM((APER, trace_rows), jnp.int32),
            pltpu.VMEM((trace_rows,), jnp.int32),
            pltpu.VMEM((trace_rows,), jnp.int32),
            pltpu.VMEM((CHUNKS, samples, PATTERNS * width), BF16),
            pltpu.VMEM((PATTERNS * trace_rows, ROWS), BF16),
            pltpu.VMEM((ROWS, PATTERNS * trace_rows), BF16),
            pltpu.VMEM((PATTERNS * trace_rows, width), BF16),
            pltpu.VMEM((PATTERNS * trace_rows, width), BF16),
            pltpu.VMEM((CHUNKS, OWN, width), F32),
            pltpu.VMEM((2, CHUNKS, AWAY, width), BF16),
            pltpu.VMEM((2, CHUNKS, AWAY, width), BF16),
            pltpu.VMEM((CHUNKS, AWAY, width), F32),
            pltpu.VMEM((CHUNKS, AWAY, width), F32),
            pltpu.VMEM((2, CHUNKS, ROWS, width), BF16),
            pltpu.VMEM((2, CHUNKS, AWAY, width), BF16),
            pltpu.VMEM((OWN, samples), F32),
            pltpu.VMEM((OWN, samples), F32),
            pltpu.VMEM((OWN, samples), F32),
            pltpu.VMEM((2, 2, CELLS, samples), F32),
            pltpu.VMEM((2, 2, CELLS, samples), F32),
            pltpu.VMEM((2, 2, 8, 128), F32),
            pltpu.VMEM((2, 2, max(n_z * 2, n_y * n_off // 2), 128), F32),
            pltpu.SemaphoreType.DMA((PATTERNS,)),
            pltpu.SemaphoreType.DMA((6,)),
            pltpu.SemaphoreType.DMA((3,)),
            pltpu.SemaphoreType.DMA((3, CHUNKS)),
            pltpu.SemaphoreType.DMA((3, CHUNKS)),
            pltpu.SemaphoreType.DMA((2, CHUNKS)),
            pltpu.SemaphoreType.DMA((2, CHUNKS)),
            pltpu.SemaphoreType.DMA((2, 2)),
            pltpu.SemaphoreType.DMA((2, 2)),
            pltpu.SemaphoreType.DMA((2, 2)),
            pltpu.SemaphoreType.DMA((2, 2)),
            pltpu.SemaphoreType.REGULAR((3,)),
        ],
        compiler_params=pltpu.CompilerParams(
            collective_id=0, has_side_effects=True, vmem_limit_bytes=60 * 2**20
        ),
        name="inversion",
    )(traces, kernels, send_list, aper_slot, aper_pattern, trace_bin, trace_count)
    shape = jax.ShapeDtypeStruct((CELLS, BINS, samples), F32)
    return pl.pallas_call(
        combine,
        out_shape=(shape, shape),
        in_specs=[vmem] * 4,
        out_specs=(vmem, vmem),
        compiler_params=pltpu.CompilerParams(vmem_limit_bytes=60 * 2**20),
        name="combine",
    )(r, z, image, weights)


def solution(mesh):
    n_mid, n_off = mesh.shape["mid"], mesh.shape["off"]
    n_z = 16 if n_mid % 16 == 0 else 4
    in_specs = (
        P(("mid", "off"), None),
        P(),
        P("mid", None, None),
        P(None, ("mid", "off")),
        P(None, ("mid", "off")),
        P(("mid", "off")),
        P(("mid", "off")),
    )
    out_specs = (P("mid", "off", None), P("mid", "off", None))
    return jax.shard_map(
        functools.partial(shards, (n_mid, n_off, n_z)),
        mesh=mesh,
        in_specs=in_specs,
        out_specs=out_specs,
        check_vma=False,
    )
```

```python
import functools

import jax
import jax.numpy as jnp
from jax import lax
from jax.experimental import pallas as pl
from jax.experimental.pallas import tpu as pltpu
from jax.sharding import PartitionSpec as P

MESH = pl.DeviceIdType.MESH
PATTERNS = 8
APER = 8
CELLS = 8
SEND = 4
DIRS = 4
BINS = 8
OWN = CELLS * BINS
PART = SEND * BINS
AWAY = DIRS * PART
ROWS = OWN + AWAY
CHUNKS = 2
SHIFTS = (1, -1, 2, -2)
FAR_FIRST = (2, 3, 0, 1)
SHRINK = 2.0 ** -14
smooth_weight = 2.0
F32 = jnp.float32
BF16 = jnp.bfloat16


def dot(a, b):
    return jnp.dot(a, b, preferred_element_type=F32)


def dot_t(a, b):
    return lax.dot_general(a, b, (((1,), (1,)), ((), ())), preferred_element_type=F32)


def by_lanes(x):
    rows, n = x.shape
    x = x.reshape(rows // 8, 8, n).sum(0)
    x = sum(x[:, i : i + 128] for i in range(0, n, 128))
    return jnp.sum(x, axis=0, keepdims=True)


def body(
    sizes,
    traces_ref,
    kernels_ref,
    send_ref,
    slot_ref,
    pattern_ref,
    bin_ref,
    count_ref,
    first_ref,
    second_ref,
    image_ref,
    weights_ref,
    moveout,
    traces_in,
    send_in,
    slot_in,
    pattern_in,
    bin_in,
    count_in,
    turned,
    pick,
    spread_to,
    spread,
    spread_low,
    own,
    back_send,
    back_land,
    fine_send,
    fine_land,
    slots,
    ahead_send,
    field0,
    field1,
    smooth,
    edge_send,
    edge_land,
    total_send,
    total_land,
    load_sem,
    table_sem,
    store_sem,
    back_ssem,
    back_rsem,
    ahead_ssem,
    ahead_rsem,
    edge_ssem,
    edge_rsem,
    total_ssem,
    total_rsem,
    meet_sem,
):
    n_mid, n_off, n_z = sizes
    n_y, n_x = n_mid // n_z, n_off // 2
    samples = moveout.shape[2]
    trace_rows = traces_in.shape[0]
    width = samples // CHUNKS
    mid = lax.axis_index("mid")
    off = lax.axis_index("off")
    row_y, col_z = lax.div(mid, n_z), lax.rem(mid, n_z)
    col_x, core = lax.div(off, 2), lax.rem(off, 2)

    def tile_at(shift):
        return lax.rem(mid + (shift + n_mid), n_mid)

    tiles_to = [tile_at(s) for s in SHIFTS]
    tiles_back = [tile_at(-s) for s in SHIFTS]

    def farthest_first(sizes_2, where):
        pairs = [(i, j) for i in range(sizes_2[0]) for j in range(sizes_2[1]) if i or j]
        pairs.sort(key=lambda ij: -min(ij[0], sizes_2[0] - ij[0]) - min(ij[1], sizes_2[1] - ij[1]))
        return [where(i, j) for i, j in pairs]

    line = farthest_first(
        (n_z, 2), lambda i, j: (row_y * n_z + lax.rem(col_z + i, n_z), col_x * 2 + lax.rem(core + j, 2))
    )
    plane = farthest_first(
        (n_y, n_x),
        lambda i, j: (lax.rem(row_y + i, n_y) * n_z + col_z, lax.rem(col_x + j, n_x) * 2 + core),
    )
    stages = (plane, line)

    tables = [
        pltpu.make_async_copy(src, dst, table_sem.at[i])
        for i, (src, dst) in enumerate(
            (
                (slot_ref, slot_in),
                (pattern_ref, pattern_in),
                (bin_ref, bin_in),
                (count_ref, count_in),
                (send_ref, send_in),
                (traces_ref, traces_in),
            )
        )
    ]
    loads = [
        pltpu.make_async_copy(kernels_ref.at[p], moveout.at[p], load_sem.at[p]) for p in range(PATTERNS)
    ]

    barrier = pltpu.get_barrier_semaphore()

    def greet(devices):
        for device in devices:
            pl.semaphore_signal(barrier, inc=1, device_id=device, device_id_type=MESH)

    def around(count, steps):
        return sorted({d % count for step in steps for d in (step, -step)} - {0})

    def at_z(steps):
        return [(row_y * n_z + lax.rem(col_z + d, n_z), off) for d in around(n_z, steps)]

    def at_y(steps):
        return [(lax.rem(row_y + d, n_y) * n_z + col_z, off) for d in around(n_y, steps)]

    def at_x(steps):
        return [(mid, lax.rem(col_x + d, n_x) * 2 + core) for d in around(n_x, steps)]

    partner = [(mid, col_x * 2 + 1 - core)]
    near = [(tile, off) for tile in tiles_to]
    near += [(mid, lax.rem(off + 1, n_off)), (mid, lax.rem(off + n_off - 1, n_off))]
    near += at_z((1, 2)) + at_y((1,)) + at_x((1,)) + partner
    rounds = (at_z((2,)) + at_y((1,)) + at_x((1,)), at_z((4,)) + at_y((2,)), at_x((1, 2)) + partner)

    def meet(i):
        for device in rounds[i]:
            pl.semaphore_signal(meet_sem.at[i], inc=1, device_id=device, device_id_type=MESH)

    def met(i):
        if rounds[i]:
            pl.semaphore_wait(meet_sem.at[i], len(rounds[i]))

    greet(near)
    for load in tables + loads:
        load.start()
    for load in tables:
        load.wait()

    slot = slot_in[...]
    live = lax.broadcasted_iota(jnp.int32, slot.shape, 0) < count_in[...].reshape(1, trace_rows)
    for k in range(DIRS):
        source = mid - SHIFTS[k]
        here = (source >= 0) & (source < n_mid)
        inside = (slot >= CELLS + k * SEND) & (slot < CELLS + (k + 1) * SEND)
        live = live & (jnp.logical_not(inside) | here)
    code = pattern_in[...] * ROWS + slot * BINS + bin_in[...].reshape(1, trace_rows)
    code = jnp.where(live, code, -1)
    row_id = lax.broadcasted_iota(jnp.int32, (ROWS, trace_rows), 0)
    for p in range(PATTERNS):
        count = jnp.zeros((ROWS, trace_rows), F32)
        for j in range(APER):
            count = count + jnp.where(code[j : j + 1, :] - p * ROWS == row_id, 1.0, 0.0)
        spread_to[:, p * trace_rows : (p + 1) * trace_rows] = count.astype(BF16)

    def cols(c):
        return slice(c * width, (c + 1) * width)

    def back_copy(turn, c, k):
        part = pl.ds(k * PART, PART)
        return pltpu.make_async_remote_copy(
            src_ref=back_send.at[turn, c, part, :],
            dst_ref=back_land.at[turn, c, part, :],
            send_sem=back_ssem.at[turn, c],
            recv_sem=back_rsem.at[turn, c],
            device_id=(tiles_back[k], off),
            device_id_type=MESH,
        )

    def ahead_copy(turn, c, k):
        return pltpu.make_async_remote_copy(
            src_ref=ahead_send.at[turn, c, pl.ds(k * PART, PART), :],
            dst_ref=slots.at[turn, c, pl.ds(OWN + k * PART, PART), :],
            send_sem=ahead_ssem.at[turn, c],
            recv_sem=ahead_rsem.at[turn, c],
            device_id=(tiles_to[k], off),
            device_id_type=MESH,
        )

    def edge_copy(turn, side):
        step = 1 - 2 * side
        return pltpu.make_async_remote_copy(
            src_ref=edge_send.at[turn, side],
            dst_ref=edge_land.at[turn, side],
            send_sem=edge_ssem.at[turn, side],
            recv_sem=edge_rsem.at[turn, side],
            device_id=(mid, lax.rem(off + step + n_off, n_off)),
            device_id_type=MESH,
        )

    def await_bytes(ref, sem):
        pltpu.make_async_copy(ref, ref, sem).wait()

    def adjoint_chunk(turn, c, values, first=False):
        groups = 2 if first else 1
        each = PATTERNS // groups
        for g in range(groups):
            if first:
                if c == 0:
                    for load in loads[g * each : (g + 1) * each]:
                        load.wait()
                wide = dot_t(values, moveout[g * each : (g + 1) * each, cols(c), :].reshape(each * width, samples))
            else:
                wide = dot(values, turned[c])
            wide = wide.astype(BF16)
            for i in range(each):
                p = g * each + i
                spread[p * trace_rows : (p + 1) * trace_rows, :] = wide[:, i * width : (i + 1) * width]
        sums = dot(spread_to[...], spread[...])
        own[c] = sums[:OWN]
        back_send[turn, c] = sums[OWN:].astype(BF16)
        if first and c == 0:
            pl.semaphore_wait(barrier, len(near))
        for k in FAR_FIRST:
            back_copy(turn, c, k).start()
        return sums

    def halves(x):
        high = x.astype(BF16)
        return high, (x - high.astype(F32)).astype(BF16)

    def fine_copy(c, k):
        part = pl.ds(k * PART, PART)
        return pltpu.make_async_remote_copy(
            src_ref=fine_send.at[c, part, :],
            dst_ref=fine_land.at[c, part, :],
            send_sem=back_ssem.at[2, c],
            recv_sem=back_rsem.at[2, c],
            device_id=(tiles_back[k], off),
            device_id_type=MESH,
        )

    def fine_chunk(c, values):
        high, low = halves(values)
        wide = halves(dot(high, turned[c]) + dot(low, turned[c]))
        for p in range(PATTERNS):
            rows = slice(p * trace_rows, (p + 1) * trace_rows)
            for part, to in zip(wide, (spread, spread_low)):
                to[rows, :] = part[:, p * width : (p + 1) * width]
        sums = dot(spread_to[...], spread[...]) + dot(spread_to[...], spread_low[...])
        own[c] = sums[:OWN]
        fine_send[c] = sums[OWN:]
        for k in FAR_FIRST:
            fine_copy(c, k).start()

    def fine_landed(c):
        await_bytes(fine_land.at[c], back_rsem.at[2, c])
        high, low = halves(fine_land[c])
        return own[c] + (dot(land_at, high) + dot(land_at, low))

    def landed(turn, c):
        await_bytes(back_land.at[turn, c], back_rsem.at[turn, c])
        return own[c] + dot(land_at, back_land[turn, c])

    def ahead_chunk(turn, c, part, field):
        rounded = part.astype(BF16)
        ahead_send[turn, c] = dot(take_from, rounded).astype(BF16)
        for k in FAR_FIRST:
            ahead_copy(turn, c, k).start()
        slots[turn, c, :OWN, :] = rounded
        field[:, cols(c)] = part

    def send_edges(turn, field):
        cube = field[...].reshape(CELLS, BINS, samples)
        edge_send[turn, 0] = cube[:, BINS - 1, :]
        edge_send[turn, 1] = cube[:, 0, :]
        for side in range(2):
            edge_copy(turn, side).start()

    def smoothed(turn, field):
        for side in range(2):
            await_bytes(edge_land.at[turn, side], edge_rsem.at[turn, side])
        before = jnp.where(off == 0, 0.0, edge_land[turn, 0])
        after = jnp.where(off == n_off - 1, 0.0, edge_land[turn, 1])
        cube = field[...].reshape(CELLS, BINS, samples)
        padded = jnp.concatenate([before[:, None, :], cube, after[:, None, :]], axis=1)
        out = smooth_weight * (2.0 * cube - padded[:, :-2] - padded[:, 2:])
        return out.reshape(OWN, samples)

    def forward(turn):
        out = None
        for c in range(CHUNKS):
            await_bytes(slots.at[turn, c, pl.ds(OWN, AWAY), :], ahead_rsem.at[turn, c])
            sums = dot(pick[...], slots[turn, c]).astype(BF16)
            wide = jnp.concatenate([sums[p * trace_rows : (p + 1) * trace_rows] for p in range(PATTERNS)], axis=1)
            part = dot(wide, moveout[:, cols(c), :].reshape(PATTERNS * width, samples))
            out = part if out is None else out + part
        return out

    def total_rows(turn, stage):
        return total_land.at[turn, stage, pl.ds(0, len(stages[stage])), :]

    def total_start(turn, stage, mine):
        total_send[turn, stage, 0:1, :] = mine
        for d, device in enumerate(stages[stage]):
            pltpu.make_async_remote_copy(
                src_ref=total_send.at[turn, stage, pl.ds(0, 1), :],
                dst_ref=total_land.at[turn, stage, pl.ds(d, 1), :],
                send_sem=total_ssem.at[turn, stage],
                recv_sem=total_rsem.at[turn, stage],
                device_id=device,
                device_id_type=MESH,
            ).start()

    def total_end(turn, stage):
        await_bytes(total_rows(turn, stage), total_rsem.at[turn, stage])
        heard = total_land[turn, stage, 0 : len(stages[stage]), :]
        return total_send[turn, stage, 0:1, :] + jnp.sum(heard, axis=0, keepdims=True)

    lane = lax.broadcasted_iota(jnp.int32, (1, 128), 1)

    def packed(row, i, part):
        part = part + pltpu.roll(part, 64, 1)
        part = part + pltpu.roll(part, 32, 1)
        return jnp.where(lane // 32 == i, part, row)

    def unpacked(row, i):
        return jnp.sum(jnp.where(lane // 32 == i, row, 0.0), axis=1, keepdims=True)

    stores = [
        pltpu.make_async_copy(src, dst, store_sem.at[i])
        for i, (src, dst) in enumerate(((field0, first_ref), (field1, second_ref), (smooth, image_ref)))
    ]

    values = traces_in[...]
    for c in range(CHUNKS):
        adjoint_chunk(0, c, values, first=True)
    meet(0)

    for p in range(PATTERNS):
        rows = slice(p * trace_rows, (p + 1) * trace_rows)
        pick[rows, :] = spread_to[:, rows].astype(F32).T.astype(BF16)

    entry = lax.broadcasted_iota(jnp.int32, (OWN, AWAY), 1)
    listed = jnp.zeros((OWN, AWAY), jnp.int32)
    for k in range(DIRS):
        for m in range(SEND):
            listed = jnp.where(entry // BINS == k * SEND + m, send_in[0, k : k + 1, m : m + 1], listed)
    place = listed * BINS + entry % BINS
    land_f32 = jnp.where(place == lax.broadcasted_iota(jnp.int32, (OWN, AWAY), 0), 1.0, 0.0)
    land_at = land_f32.astype(BF16)
    take_from = land_f32.T.astype(BF16)

    for c in range(CHUNKS):
        for p in range(PATTERNS):
            turned[c, :, p * width : (p + 1) * width] = moveout[p, cols(c), :].T
    met(0)
    meet(1)
    norm = jnp.zeros((1, 128), F32)
    for c in range(CHUNKS):
        part = landed(0, c)
        ahead_chunk(0, c, part, field0)
        norm = norm + by_lanes(part * part)
    norm_r = norm

    send_edges(0, field0)
    stores[0].start()
    smooth[...] = smoothed(0, field0)
    cross = by_lanes(field0[...] * smooth[...])
    met(1)
    meet(2)
    values = forward(0).astype(BF16)
    heard = values.astype(F32)
    curve_r = by_lanes(heard * heard) + cross
    for c in range(CHUNKS):
        adjoint_chunk(1, c, values)
    norm = jnp.zeros((1, 128), F32)
    for c in range(CHUNKS):
        part = (landed(1, c) + smooth[:, cols(c)]) * SHRINK
        ahead_chunk(1, c, part, field1)
        norm = norm + by_lanes(part * part)

    send_edges(1, field1)
    stores[1].start()
    smooth[...] = smoothed(1, field1)
    cross = by_lanes(field1[...] * smooth[...])
    sums = jnp.zeros((1, 128), F32)
    for i, part in enumerate((curve_r, norm, norm_r)):
        sums = packed(sums, i, part)
    met(2)
    heard = forward(1)
    total_start(1, 0, packed(sums, 3, by_lanes(heard * heard) + cross))
    for c in range(CHUNKS):
        fine_chunk(c, heard)
    total_start(1, 1, total_end(1, 0))
    for c in range(CHUNKS):
        smooth[:, cols(c)] = fine_landed(c) + smooth[:, cols(c)]
    stores[2].start()
    sums = total_end(1, 1)
    ra, zz, rr, za = (unpacked(sums, i) for i in range(4))

    grow = 1.0 / SHRINK
    step_0, one_over = rr / ra, 1.0 / rr
    scaled = step_0 * grow
    norm_1 = scaled * (scaled * zz) - rr
    more = 1.0 + norm_1 * one_over
    curve_1 = more * (more * ra) - 2.0 * more * (scaled * (zz * grow)) + scaled * (scaled * za)
    step_1 = norm_1 / curve_1
    along = step_1 * more
    row = lax.broadcasted_iota(jnp.int32, (8, 128), 0)
    weights = jnp.zeros((8, 128), F32)
    for i, weight in enumerate(
        (step_0 + along, -(step_1 * scaled), jnp.ones_like(rr), -(scaled + along * grow), step_1 * scaled)
    ):
        weights = jnp.where(row == i, weight, weights)
    weights_ref[...] = weights
    for store in stores:
        store.wait()

    for c in range(CHUNKS):
        for turn in range(2):
            await_bytes(back_send.at[turn, c], back_ssem.at[turn, c])
            await_bytes(ahead_send.at[turn, c], ahead_ssem.at[turn, c])
        await_bytes(fine_send.at[c], back_ssem.at[2, c])
    for turn in range(2):
        for side in range(2):
            await_bytes(edge_send.at[turn, side], edge_ssem.at[turn, side])
    for stage in range(2):
        await_bytes(total_rows(1, stage), total_ssem.at[1, stage])


def combine(r_ref, z_ref, image_ref, weights_ref, solution_ref, residual_ref):
    weight = [weights_ref[i : i + 1, 0:1] for i in range(5)]
    r, z = r_ref[...], z_ref[...]
    solution_ref[...] = (weight[0] * r + weight[1] * z).reshape(solution_ref.shape)
    left = weight[2] * r + weight[3] * z + weight[4] * image_ref[...]
    residual_ref[...] = left.reshape(residual_ref.shape)


def shards(sizes, traces, kernels, send_list, aper_slot, aper_pattern, trace_bin, trace_count):
    n_mid, n_off, n_z = sizes
    n_y = n_mid // n_z
    trace_rows, samples = traces.shape
    width = samples // CHUNKS
    vmem = pl.BlockSpec(memory_space=pltpu.VMEM)
    hbm = pl.BlockSpec(memory_space=pltpu.HBM)
    field = jax.ShapeDtypeStruct((OWN, samples), F32)
    r, z, image, weights = pl.pallas_call(
        functools.partial(body, sizes),
        out_shape=(field, field, field, jax.ShapeDtypeStruct((8, 128), F32)),
        in_specs=[hbm] * 7,
        out_specs=(hbm, hbm, hbm, vmem),
        scratch_shapes=[
            pltpu.VMEM((PATTERNS, samples, samples), BF16),
            pltpu.VMEM((trace_rows, samples), BF16),
            pltpu.VMEM(send_list.shape, jnp.int32),
            pltpu.VMEM((APER, trace_rows), jnp.int32),
            pltpu.VMEM((APER, trace_rows), jnp.int32),
            pltpu.VMEM((trace_rows,), jnp.int32),
            pltpu.VMEM((trace_rows,), jnp.int32),
            pltpu.VMEM((CHUNKS, samples, PATTERNS * width), BF16),
            pltpu.VMEM((PATTERNS * trace_rows, ROWS), BF16),
            pltpu.VMEM((ROWS, PATTERNS * trace_rows), BF16),
            pltpu.VMEM((PATTERNS * trace_rows, width), BF16),
            pltpu.VMEM((PATTERNS * trace_rows, width), BF16),
            pltpu.VMEM((CHUNKS, OWN, width), F32),
            pltpu.VMEM((2, CHUNKS, AWAY, width), BF16),
            pltpu.VMEM((2, CHUNKS, AWAY, width), BF16),
            pltpu.VMEM((CHUNKS, AWAY, width), F32),
            pltpu.VMEM((CHUNKS, AWAY, width), F32),
            pltpu.VMEM((2, CHUNKS, ROWS, width), BF16),
            pltpu.VMEM((2, CHUNKS, AWAY, width), BF16),
            pltpu.VMEM((OWN, samples), F32),
            pltpu.VMEM((OWN, samples), F32),
            pltpu.VMEM((OWN, samples), F32),
            pltpu.VMEM((2, 2, CELLS, samples), F32),
            pltpu.VMEM((2, 2, CELLS, samples), F32),
            pltpu.VMEM((2, 2, 8, 128), F32),
            pltpu.VMEM((2, 2, max(n_z * 2, n_y * n_off // 2), 128), F32),
            pltpu.SemaphoreType.DMA((PATTERNS,)),
            pltpu.SemaphoreType.DMA((6,)),
            pltpu.SemaphoreType.DMA((3,)),
            pltpu.SemaphoreType.DMA((3, CHUNKS)),
            pltpu.SemaphoreType.DMA((3, CHUNKS)),
            pltpu.SemaphoreType.DMA((2, CHUNKS)),
            pltpu.SemaphoreType.DMA((2, CHUNKS)),
            pltpu.SemaphoreType.DMA((2, 2)),
            pltpu.SemaphoreType.DMA((2, 2)),
            pltpu.SemaphoreType.DMA((2, 2)),
            pltpu.SemaphoreType.DMA((2, 2)),
            pltpu.SemaphoreType.REGULAR((3,)),
        ],
        compiler_params=pltpu.CompilerParams(
            collective_id=0, has_side_effects=True, vmem_limit_bytes=60 * 2**20
        ),
        name="inversion",
    )(traces, kernels, send_list, aper_slot, aper_pattern, trace_bin, trace_count)
    shape = jax.ShapeDtypeStruct((CELLS, BINS, samples), F32)
    return pl.pallas_call(
        combine,
        out_shape=(shape, shape),
        in_specs=[vmem] * 4,
        out_specs=(vmem, vmem),
        compiler_params=pltpu.CompilerParams(vmem_limit_bytes=60 * 2**20),
        name="combine",
    )(r, z, image, weights)


def solution(mesh):
    n_mid, n_off = mesh.shape["mid"], mesh.shape["off"]
    n_z = 16 if n_mid % 16 == 0 else 4
    in_specs = (
        P(("mid", "off"), None),
        P(),
        P("mid", None, None),
        P(None, ("mid", "off")),
        P(None, ("mid", "off")),
        P(("mid", "off")),
        P(("mid", "off")),
    )
    out_specs = (P("mid", "off", None), P("mid", "off", None))
    return jax.shard_map(
        functools.partial(shards, (n_mid, n_off, n_z)),
        mesh=mesh,
        in_specs=in_specs,
        out_specs=out_specs,
        check_vma=False,
    )
```
